256 devices in a mesh: tm: 32 (over z, y), dp: 8 (over x, core).
Axes of the slice: x: 4, y: 4, z: 8, core: 2. Of those that a mesh axis runs over, the one named last changes fastest.
Arguments:
- inputs: bfloat16 [8, 32768, 1024], P('dp', 'tm'), may hold values from -6 to 6
- weights: bfloat16 [1024, 1536], replicated, may hold values from -0.1875 to 0.1875
- out_grad: bfloat16 [8, 32768, 512], P('dp', 'tm'), may hold values from -6 to 6
Outputs:
- input_grad: bfloat16 [8, 32768, 1024], P('dp', 'tm')
- weight_grad: float32 [1024, 1536], P('tm')
The draws below stay inside these ranges and needn't reach their ends.
All inputs are finite; a program needn't handle non-finite values.
Results may differ from the reference program's by a relative error of at most 0.0075.
Values sent between devices are 32-bit elements; how exact they have to be, the bound alone decides.
No kernel may reach another device: no remote copies, remote signals or barrier semaphores. Data moves between devices by JAX's collectives and lax.ppermute only.
A program may use at most 128 MiB of HBM per device.

```python
import jax
import jax.numpy as jnp
from jax import lax

DM = 1024
H = 4
HD = 128
D = 512
CH = 256
TOKENS = 32768
REC = 8


def level_of(stream_key, dims, split, low, top_value):
    def one(dim, parts):
        draws = jax.random.uniform(jax.random.fold_in(jax.random.fold_in(stream_key, 6), dim), (parts,), jnp.float32, low / len(split), top_value / len(split))
        return jnp.repeat(jnp.exp(draws), dims[dim] // parts).reshape((-1,) + (1,) * (len(dims) - dim - 1))

    factor_of = one(*split[0])
    for cut in split[1:]:
        factor_of = factor_of * one(*cut)
    return factor_of


def normal_values(stream_key, shape, scale, most, split=(), kind=jnp.bfloat16):
    drawn = jax.random.normal(stream_key, shape, jnp.float32) * scale
    if len(split) > 0:
        drawn = level_of(stream_key, shape, split, -0.22, 0.18) * drawn
    return jnp.clip(drawn, min=-most, max=most).astype(kind)


def setup_inputs(seed: int = 0) -> dict:
    key_of = jax.random.split(jax.random.key(seed), 4)
    return {
        "inputs": normal_values(key_of[0], (REC, TOKENS, DM), 1.0, 6.0, ((0, 8), (1, 32))),
        "weights": normal_values(key_of[1], (DM, 3 * D), DM ** -0.5, 0.1875),
        "out_grad": normal_values(key_of[2], (REC, TOKENS, D), 1.0, 6.0, ((0, 8), (1, 32))),
    }


def group_grads(queries, key_rows, values, scaled_grad, state_start, grad_end):
    hi = lax.Precision.HIGHEST
    tri = (lax.broadcasted_iota(jnp.int32, (CH, CH), 0) >= lax.broadcasted_iota(jnp.int32, (CH, CH), 1)).astype(jnp.float32)
    kv_group = jnp.einsum('nshd,nshe->nhde', key_rows, values, precision=hi)
    qg_group = jnp.einsum('nthd,nthe->nhde', queries, scaled_grad, precision=hi)
    state_before = (state_start[None] + jnp.cumsum(kv_group, 0) - kv_group).astype(jnp.bfloat16).astype(jnp.float32)
    grad_after = (grad_end[None] + jnp.flip(jnp.cumsum(jnp.flip(qg_group, 0), 0), 0) - qg_group).astype(jnp.bfloat16).astype(jnp.float32)
    mix_vg = (jnp.einsum('nthe,nshe->nhts', scaled_grad, values, precision=hi) * tri).astype(jnp.bfloat16).astype(jnp.float32)
    mix_qk = (jnp.einsum('nthd,nshd->nhts', queries, key_rows, precision=hi) * tri).astype(jnp.bfloat16).astype(jnp.float32)
    grad_q = jnp.einsum('nhts,nshd->nthd', mix_vg, key_rows, precision=hi) + jnp.einsum('nthe,nhde->nthd', scaled_grad, state_before, precision=hi)
    grad_k = jnp.einsum('nhts,nthd->nshd', mix_vg, queries, precision=hi) + jnp.einsum('nshe,nhde->nshd', values, grad_after, precision=hi)
    grad_v = jnp.einsum('nhts,nthe->nshe', mix_qk, scaled_grad, precision=hi) + jnp.einsum('nshd,nhde->nshe', key_rows, grad_after, precision=hi)
    return (grad_q, grad_k, grad_v)

def reference(inputs, weights, out_grad):
    width = H * HD

    def one_recording(pair):
        record, cotangent = pair
        qkv = jnp.dot(record, weights, preferred_element_type=jnp.float32).astype(jnp.bfloat16)
        shape4 = (TOKENS // CH, CH, H, HD)
        queries = qkv[:, :width].astype(jnp.float32).reshape(shape4)
        key_rows = qkv[:, width:2 * width].astype(jnp.float32).reshape(shape4)
        values = qkv[:, 2 * width:].astype(jnp.float32).reshape(shape4)
        position = jnp.arange(TOKENS, dtype=jnp.int32).astype(jnp.float32)
        factor = 1.0 / jnp.sqrt(jnp.float32(HD) * (position + 1.0))
        scaled_grad = (cotangent.astype(jnp.float32) * factor[:, None]).astype(jnp.bfloat16).astype(jnp.float32).reshape(shape4)
        zeros = jnp.zeros((H, HD, HD), jnp.float32)
        grad_q, grad_k, grad_v = group_grads(queries, key_rows, values, scaled_grad, zeros, zeros)
        dqkv = jnp.concatenate([grad_q.reshape(TOKENS, width), grad_k.reshape(TOKENS, width), grad_v.reshape(TOKENS, width)], axis=1).astype(jnp.bfloat16)
        record_grad = lax.dot_general(dqkv, weights, (((1,), (1,)), ((), ())), preferred_element_type=jnp.float32).astype(jnp.bfloat16)
        proj_grad = lax.dot_general(record, dqkv, (((0,), (0,)), ((), ())), preferred_element_type=jnp.float32)
        return (record_grad, proj_grad)
    input_grad, proj_parts = lax.map(one_recording, (inputs, out_grad))
    return (input_grad, lax.optimization_barrier(jnp.sum(proj_parts, 0)))
```

```python
import functools

import jax
import jax.numpy as jnp
from jax import lax
from jax.experimental import pallas as pl
from jax.experimental.pallas import tpu as pltpu
from jax.sharding import Mesh, PartitionSpec as P

H = 4
HD = 128
CH = 256
NB = 4
D = H * HD
DM = 1024
TOK = NB * CH
F32 = jnp.float32
BF16 = jnp.bfloat16

NN = (((1,), (0,)), ((), ()))
NT = (((1,), (1,)), ((), ()))
TN = (((0,), (0,)), ((), ()))


def dot(a, b, dims):
    return lax.dot_general(a, b, dims, preferred_element_type=F32)


def params():
    return pltpu.CompilerParams(vmem_limit_bytes=56 * 1024 * 1024)


def head(part, h):
    return pl.ds(part * D + h * HD, HD)


def project_body(pos_ref, x_ref, w_ref, g_ref, qkv_ref, sg_ref, xt_ref, kv_ref, qg_ref, total_ref):
    n = pl.program_id(0)
    qkv_ref[...] = dot(x_ref[...], w_ref[...], NN).astype(BF16)
    pos = (pos_ref[0] + n * CH + lax.broadcasted_iota(jnp.int32, (CH, 1), 0)).astype(F32)
    factor = 1.0 / jnp.sqrt(jnp.float32(HD) * (pos + 1.0))
    sg_ref[...] = (g_ref[...].astype(F32) * factor).astype(BF16)
    xt_ref[...] = x_ref[...].T

    @pl.when(n == 0)
    def _():
        total_ref[...] = jnp.zeros_like(total_ref)

    for h in range(H):
        kv = dot(qkv_ref[:, head(1, h)], qkv_ref[:, head(2, h)], TN)
        qg = dot(qkv_ref[:, head(0, h)], sg_ref[:, pl.ds(h * HD, HD)], TN)
        kv_ref[0, h] = kv
        qg_ref[0, h] = qg
        total_ref[0, h] += kv
        total_ref[1, h] += qg


def project(offset, x, w, g):
    block = lambda cols: pl.BlockSpec((CH, cols), lambda n, s: (n, 0))
    sums = pl.BlockSpec((1, H, HD, HD), lambda n, s: (n, 0, 0, 0))
    return pl.pallas_call(
        project_body,
        grid_spec=pltpu.PrefetchScalarGridSpec(
            num_scalar_prefetch=1,
            grid=(NB,),
            in_specs=[block(DM), pl.BlockSpec((DM, 3 * D), lambda n, s: (0, 0)), block(D)],
            out_specs=[
                block(3 * D),
                block(D),
                pl.BlockSpec((DM, CH), lambda n, s: (0, n)),
                sums,
                sums,
                pl.BlockSpec((2, H, HD, HD), lambda n, s: (0, 0, 0, 0)),
            ],
        ),
        out_shape=[
            jax.ShapeDtypeStruct((TOK, 3 * D), BF16),
            jax.ShapeDtypeStruct((TOK, D), BF16),
            jax.ShapeDtypeStruct((DM, TOK), BF16),
            jax.ShapeDtypeStruct((NB, H, HD, HD), F32),
            jax.ShapeDtypeStruct((NB, H, HD, HD), F32),
            jax.ShapeDtypeStruct((2, H, HD, HD), F32),
        ],
        compiler_params=params(),
        name="project",
    )(offset, x, w, g)


def scan_body(count, back_ref, v_ref, o_ref):
    def step(t, so_far):
        i = jnp.where(back_ref[0] == 1, count - 1 - t, t)
        o_ref[i] = so_far
        return so_far + v_ref[i]

    lax.fori_loop(0, count, step, jnp.zeros(v_ref.shape[1:], F32))


def scan_states(back, v):
    return pl.pallas_call(
        functools.partial(scan_body, v.shape[0]),
        in_specs=[pl.BlockSpec(memory_space=pltpu.SMEM), pl.BlockSpec(memory_space=pltpu.VMEM)],
        out_specs=pl.BlockSpec(memory_space=pltpu.VMEM),
        out_shape=jax.ShapeDtypeStruct(v.shape, F32),
        compiler_params=params(),
        name="scan_states",
    )(back, v)


def grads_body(qkv_ref, sg_ref, kv_ref, qg_ref, s_ref, o_ref):
    n = pl.program_id(0)
    keep = lax.broadcasted_iota(jnp.int32, (CH, CH), 0) >= lax.broadcasted_iota(jnp.int32, (CH, CH), 1)
    for h in range(H):
        q, k, v = (qkv_ref[:, head(p, h)] for p in range(3))
        g = sg_ref[:, pl.ds(h * HD, HD)]
        before = s_ref[0, h]
        after = s_ref[1, h]
        for m in range(NB):
            before = before + jnp.where(m < n, kv_ref[m, h], 0.0)
            after = after + jnp.where(m > n, qg_ref[m, h], 0.0)
        before = before.astype(BF16)
        after = after.astype(BF16)
        mvg = jnp.where(keep, dot(g, v, NT), 0.0).astype(BF16)
        mqk = jnp.where(keep, dot(q, k, NT), 0.0).astype(BF16)
        dq = dot(mvg, k, NN) + dot(g, before, NT)
        dk = dot(mvg, q, TN) + dot(v, after, NT)
        dv = dot(mqk, g, TN) + dot(k, after, NN)
        for p, d in enumerate((dq, dk, dv)):
            o_ref[:, head(p, h)] = d.astype(BF16)


def grads(qkv, sg, kv, qg, states):
    block = lambda cols: pl.BlockSpec((CH, cols), lambda n: (n, 0))
    sums = pl.BlockSpec((NB, H, HD, HD), lambda n: (0, 0, 0, 0))
    return pl.pallas_call(
        grads_body,
        grid=(NB,),
        in_specs=[block(3 * D), block(D), sums, sums, pl.BlockSpec((2, H, HD, HD), lambda n: (0, 0, 0, 0))],
        out_specs=block(3 * D),
        out_shape=jax.ShapeDtypeStruct((TOK, 3 * D), BF16),
        compiler_params=params(),
        name="grads",
    )(qkv, sg, kv, qg, states)


def give_body(at_ref, xt_ref, d_ref, o_ref):
    o_ref[...] = dot(xt_ref[...], d_ref[...], NN)


def give_half(at, xt, dqkv):
    return pl.pallas_call(
        give_body,
        grid_spec=pltpu.PrefetchScalarGridSpec(
            num_scalar_prefetch=1,
            grid=(3,),
            in_specs=[
                pl.BlockSpec((DM, TOK), lambda j, s: (0, 0)),
                pl.BlockSpec((TOK, 256), lambda j, s: (0, 2 * j + 1 - s[0])),
            ],
            out_specs=pl.BlockSpec((DM, 256), lambda j, s: (0, j)),
        ),
        out_shape=jax.ShapeDtypeStruct((DM, 768), F32),
        compiler_params=params(),
        name="give_half",
    )(at, xt, dqkv)


def pick(at_ref, axis):
    mine, far, first, second = (at_ref[1 + 4 * axis + i] for i in range(4))
    return (mine, second), (first, far)


def keep_body(at_ref, xt_ref, d_ref, r_ref, kx_ref, sx_ref, ky_ref, sy_ref, s_ref):
    s_ref[...] = (dot(xt_ref[...], d_ref[...], NN) + r_ref[...]).reshape(8, 4, 4, 8, 256)
    kept, sent = pick(at_ref, 0)
    for i in range(2):
        kx_ref[:, :, i] = s_ref[:, :, kept[i], :, 0:128]
        sx_ref[:, :, i] = s_ref[:, :, sent[i], :, 0:128]
    kept, sent = pick(at_ref, 1)
    for i in range(2):
        ky_ref[:, i] = s_ref[:, kept[i], :, :, 128:256]
        sy_ref[:, i] = s_ref[:, sent[i], :, :, 128:256]


def keep_half(at, xt, dqkv, arrived):
    bx = pl.BlockSpec((8, 4, 2, 8, 128), lambda j, s: (0, 0, 0, 0, j))
    by = pl.BlockSpec((8, 2, 4, 8, 128), lambda j, s: (0, 0, 0, 0, j))
    return pl.pallas_call(
        keep_body,
        grid_spec=pltpu.PrefetchScalarGridSpec(
            num_scalar_prefetch=1,
            grid=(3,),
            in_specs=[
                pl.BlockSpec((DM, TOK), lambda j, s: (0, 0)),
                pl.BlockSpec((TOK, 256), lambda j, s: (0, 2 * j + s[0])),
                pl.BlockSpec((DM, 256), lambda j, s: (0, j)),
            ],
            out_specs=[bx, bx, by, by],
            scratch_shapes=[pltpu.VMEM((8, 4, 4, 8, 256), F32)],
        ),
        out_shape=[jax.ShapeDtypeStruct((8, 4, 2, 8, 384), F32)] * 2
        + [jax.ShapeDtypeStruct((8, 2, 4, 8, 384), F32)] * 2,
        compiler_params=params(),
        name="keep_half",
    )(at, xt, dqkv, arrived)


def whole_call(body, name, shapes, *args, scratch=()):
    vmem = pl.BlockSpec(memory_space=pltpu.VMEM)
    smem = pl.BlockSpec(memory_space=pltpu.SMEM)
    return pl.pallas_call(
        body,
        in_specs=[smem if a.dtype == jnp.int32 else vmem for a in args],
        out_specs=[vmem] * len(shapes),
        out_shape=[jax.ShapeDtypeStruct(s, F32) for s in shapes],
        scratch_shapes=list(scratch),
        compiler_params=params(),
        name=name,
    )(*args)


def add1_body(kx, rx, ky, ry, kx2, sx2, ky2, sy2):
    kx2[...] = kx[:, :, 0] + rx[:, :, 0]
    sx2[...] = kx[:, :, 1] + rx[:, :, 1]
    ky2[...] = ky[:, 0] + ry[:, 0]
    sy2[...] = ky[:, 1] + ry[:, 1]


def add2_body(at, kx, rx, ky, ry, kp, sp, kq, sq):
    for axis, k, r, ko, so in ((1, kx, rx, kp, sp), (0, ky, ry, kq, sq)):
        kept, sent = pick(at, axis)
        for i in range(2):
            ko[:, i] = k[:, kept[i]] + r[:, kept[i]]
            so[:, i] = k[:, sent[i]] + r[:, sent[i]]


def add3_body(kp, rp, kq, rq, kp2, sp2, kq2, sq2):
    for k, r, ko, so in ((kp, rp, kp2, sp2), (kq, rq, kq2, sq2)):
        ko[...] = k[:, 0] + r[:, 0]
        so[...] = k[:, 1] + r[:, 1]


def add4_body(kp, rp, kq, rq, o):
    o[:, :, 0:384] = kp[...] + rp[...]
    o[:, :, 384:768] = kq[...] + rq[...]


def sum_body(v, o):
    total = v[0]
    for i in range(1, v.shape[0]):
        total = total + v[i]
    o[...] = total


def rows_body(at, a0, a1, a2, a3, o):
    x = at[1]
    for d, a in enumerate((a0, a1, a2, a3)):
        o[(x + 4 - d) % 4] = a[...]


def columns_body(at, mine, other, o):
    c = at[0]

    def put(core, a):
        for j in range(3):
            for half in range(2):
                value = a[:, half * 384 + j * 128 : half * 384 + (j + 1) * 128]
                o[:, j * 512 + core * 256 + half * 128 : j * 512 + core * 256 + (half + 1) * 128] = value

    @pl.when(c == 0)
    def _():
        put(0, mine[...])
        put(1, other[...])

    @pl.when(c == 1)
    def _():
        put(1, mine[...])
        put(0, other[...])


def exchange(value, axis, step):
    pairs = []
    for i in range(4):
        for c in range(2):
            j = i ^ ((1, 3), (3, 1))[c][step]
            pairs.append((2 * i + c, 2 * j + c))
    return lax.ppermute(value, (axis, "core"), pairs)


def shards(inputs, weights, out_grad):
    x = inputs[0]
    z_at, y_at, x_at, core = (lax.axis_index(a) for a in ("z", "y", "x", "core"))
    tm_at = z_at * 4 + y_at
    first = jnp.where(core == 0, 1, 3)
    second = 4 - first
    at = jnp.stack(
        [core]
        + [v for i in (x_at, y_at) for v in (i, i ^ first ^ second, i ^ first, i ^ second)]
    ).astype(jnp.int32)
    offset = (tm_at * TOK).astype(jnp.int32)[None]
    back = (tm_at >= 16).astype(jnp.int32)[None]

    qkv, sg, xt, kv, qg, total = project(offset, x, weights, out_grad[0])
    slices = lax.all_to_all(total.reshape(32, 32, HD), ("z", "y"), 0, 0, tiled=True)
    states = lax.all_to_all(scan_states(back, slices), ("z", "y"), 0, 0, tiled=True)
    dqkv = grads(qkv, sg, kv, qg, states.reshape(2, H, HD, HD))

    given = give_half(at, xt, dqkv)
    arrived = lax.ppermute(given, "core", [(0, 1), (1, 0)])
    record_grad = dot(dqkv, weights, NT).astype(BF16)
    arrived, record_grad = lax.optimization_barrier((arrived, record_grad))
    kx, sx, ky, sy = keep_half(at, xt, dqkv, arrived)
    rx = exchange(sx, "x", 0)
    ry = exchange(sy, "y", 0)
    kx, sx, ky, sy = whole_call(add1_body, "add1", [(8, 4, 8, 384)] * 4, kx, rx, ky, ry)
    rx = exchange(sx, "x", 1)
    ry = exchange(sy, "y", 1)
    kp, sp, kq, sq = whole_call(add2_body, "add2", [(8, 2, 8, 384)] * 4, at, kx, rx, ky, ry)
    rp = exchange(sp, "y", 0)
    rq = exchange(sq, "x", 0)
    kp, sp, kq, sq = whole_call(add3_body, "add3", [(8, 8, 384)] * 4, kp, rp, kq, rq)
    rp = exchange(sp, "y", 1)
    rq = exchange(sq, "x", 1)
    (part,) = whole_call(add4_body, "add4", [(8, 8, 768)], kp, rp, kq, rq)
    part = lax.all_to_all(part, "z", 0, 0, tiled=True)
    (mine,) = whole_call(sum_body, "sum_z", [(8, 768)], part)
    around = [mine] + [
        lax.ppermute(mine, "x", [(i, (i + d) % 4) for i in range(4)]) for d in range(1, 4)
    ]
    (rows,) = whole_call(rows_body, "rows", [(4, 8, 768)], at, *around)
    rows = rows.reshape(32, 768)
    other = lax.ppermute(rows, "core", [(0, 1), (1, 0)])
    (proj_grad,) = whole_call(columns_body, "columns", [(32, 3 * D)], at, rows, other)
    return record_grad[None], proj_grad


def solution(mesh):
    fine = Mesh(mesh.devices.reshape(8, 4, 4, 2), ("z", "y", "x", "core"))
    tm, dp = ("z", "y"), ("x", "core")
    placed = (P(dp, tm, None), P(), P(dp, tm, None))
    return jax.shard_map(
        shards,
        mesh=fine,
        in_specs=placed,
        out_specs=(P(dp, tm, None), P(tm, None)),
        check_vma=False,
    )
```

```python
import functools

import jax
import jax.numpy as jnp
from jax import lax
from jax.experimental import pallas as pl
from jax.experimental.pallas import tpu as pltpu
from jax.sharding import Mesh, PartitionSpec as P

H = 4
HD = 128
CH = 256
NB = 4
D = H * HD
DM = 1024
TOK = NB * CH
F32 = jnp.float32
BF16 = jnp.bfloat16

NN = (((1,), (0,)), ((), ()))
NT = (((1,), (1,)), ((), ()))
TN = (((0,), (0,)), ((), ()))


def dot(a, b, dims):
    return lax.dot_general(a, b, dims, preferred_element_type=F32)


MIB = 1024 * 1024
SWAP = [(0, 1), (1, 0)]


def params(mib=40):
    return pltpu.CompilerParams(vmem_limit_bytes=mib * MIB)


def cost(flops, moved):
    return pl.CostEstimate(flops=int(flops), bytes_accessed=int(moved), transcendentals=0)


def head(part, h):
    return pl.ds(part * D + h * HD, HD)


def project_body(pos_ref, x_ref, w_ref, g_ref, qkv_ref, sg_ref, kv_ref, qg_ref, total_ref):
    n = pl.program_id(0)
    qkv_ref[...] = dot(x_ref[...], w_ref[...], NN).astype(BF16)
    pos = (pos_ref[0] + n * CH + lax.broadcasted_iota(jnp.int32, (CH, 1), 0)).astype(F32)
    factor = 1.0 / jnp.sqrt(jnp.float32(HD) * (pos + 1.0))
    sg_ref[...] = (g_ref[...].astype(F32) * factor).astype(BF16)

    @pl.when(n == 0)
    def _():
        total_ref[...] = jnp.zeros_like(total_ref)

    for h in range(H):
        kv = dot(qkv_ref[:, head(1, h)], qkv_ref[:, head(2, h)], TN)
        qg = dot(qkv_ref[:, head(0, h)], sg_ref[:, pl.ds(h * HD, HD)], TN)
        kv_ref[0, h] = kv
        qg_ref[0, h] = qg
        total_ref[0, h] += kv
        total_ref[1, h] += qg


def project(offset, x, w, g):
    block = lambda cols: pl.BlockSpec((CH, cols), lambda n, s: (n, 0))
    sums = pl.BlockSpec((1, H, HD, HD), lambda n, s: (n, 0, 0, 0))
    return pl.pallas_call(
        project_body,
        grid_spec=pltpu.PrefetchScalarGridSpec(
            num_scalar_prefetch=1,
            grid=(NB,),
            in_specs=[block(DM), pl.BlockSpec((DM, 3 * D), lambda n, s: (0, 0)), block(D)],
            out_specs=[
                block(3 * D),
                block(D),
                sums,
                sums,
                pl.BlockSpec((2, H, HD, HD), lambda n, s: (0, 0, 0, 0)),
            ],
        ),
        out_shape=[
            jax.ShapeDtypeStruct((TOK, 3 * D), BF16),
            jax.ShapeDtypeStruct((TOK, D), BF16),
            jax.ShapeDtypeStruct((NB, H, HD, HD), F32),
            jax.ShapeDtypeStruct((NB, H, HD, HD), F32),
            jax.ShapeDtypeStruct((2, H, HD, HD), F32),
        ],
        compiler_params=params(),
        name="project",
    )(offset, x, w, g)


def scan_body(count, back_ref, v_ref, *refs):
    o_ref = refs[-1]

    def step(t, so_far):
        i = jnp.where(back_ref[0] == 1, count - 1 - t, t)
        o_ref[i] = so_far
        return so_far + v_ref[i]

    lax.fori_loop(0, count, step, jnp.zeros(v_ref.shape[1:], F32))


def scan_states(back, v, after):
    return pl.pallas_call(
        functools.partial(scan_body, v.shape[0]),
        in_specs=[pl.BlockSpec(memory_space=pltpu.SMEM), pl.BlockSpec(memory_space=pltpu.VMEM)]
        + [pl.BlockSpec(memory_space=pl.ANY)] * len(after),
        out_specs=pl.BlockSpec(memory_space=pltpu.VMEM),
        out_shape=jax.ShapeDtypeStruct(v.shape, F32),
        compiler_params=params(4),
        name="scan_states",
    )(back, v, *after)


def local_body(qkv_ref, sg_ref, kv_ref, qg_ref, o_ref):
    n = pl.program_id(0)
    keep = lax.broadcasted_iota(jnp.int32, (CH, CH), 0) >= lax.broadcasted_iota(jnp.int32, (CH, CH), 1)
    for h in range(H):
        q, k, v = (qkv_ref[:, head(p, h)] for p in range(3))
        g = sg_ref[:, pl.ds(h * HD, HD)]
        before = jnp.zeros((HD, HD), F32)
        after = jnp.zeros((HD, HD), F32)
        for m in range(NB):
            before = before + jnp.where(m < n, kv_ref[m, h], 0.0)
            after = after + jnp.where(m > n, qg_ref[m, h], 0.0)
        before = before.astype(BF16)
        after = after.astype(BF16)
        mvg = jnp.where(keep, dot(g, v, NT), 0.0).astype(BF16)
        mqk = jnp.where(keep, dot(q, k, NT), 0.0).astype(BF16)
        dq = dot(mvg, k, NN) + dot(g, before, NT)
        dk = dot(mvg, q, TN) + dot(v, after, NT)
        dv = dot(mqk, g, TN) + dot(k, after, NN)
        for p, d in enumerate((dq, dk, dv)):
            o_ref[:, head(p, h)] = d.astype(BF16)


def local(qkv, sg, kv, qg):
    block = lambda cols: pl.BlockSpec((CH, cols), lambda n: (n, 0))
    sums = pl.BlockSpec((NB, H, HD, HD), lambda n: (0, 0, 0, 0))
    return pl.pallas_call(
        local_body,
        grid=(NB,),
        in_specs=[block(3 * D), block(D), sums, sums],
        out_specs=block(3 * D),
        out_shape=jax.ShapeDtypeStruct((TOK, 3 * D), BF16),
        compiler_params=params(20),
        cost_estimate=cost(4e9, 20e6),
        name="local",
    )(qkv, sg, kv, qg)


def factors_body(at_ref, x_ref, g_ref, k_ref, v_ref, o_ref):
    for j, ref in enumerate((g_ref, v_ref, k_ref)):
        o_ref[:, j * 256 : (j + 1) * 256] = dot(x_ref[...], ref[...], TN).astype(o_ref.dtype)


def factors(at, x, sg, qkv, mine, kind, name):
    def cols(first):
        return pl.BlockSpec((TOK, 256), lambda i, s: (0, first + (s[0] if mine else 1 - s[0])))

    return pl.pallas_call(
        factors_body,
        grid_spec=pltpu.PrefetchScalarGridSpec(
            num_scalar_prefetch=1,
            grid=(2,),
            in_specs=[pl.BlockSpec((TOK, DM // 2), lambda i, s: (0, i)), cols(0), cols(2), cols(4)],
            out_specs=pl.BlockSpec((DM // 2, 768), lambda i, s: (i, 0)),
        ),
        out_shape=jax.ShapeDtypeStruct((DM, 768), kind),
        compiler_params=params(24),
        cost_estimate=cost(3e9, 12e6),
        name=name,
    )(at, x, sg, qkv, qkv)


def give_body(at_ref, x_ref, q_ref, k_ref, v_ref, o_ref):
    for j, ref in enumerate((q_ref, k_ref, v_ref)):
        o_ref[:, j * 256 : (j + 1) * 256] = dot(x_ref[...], ref[...], TN)


def keep_body(at_ref, x_ref, q_ref, k_ref, v_ref, r_ref, o_ref):
    for j, ref in enumerate((q_ref, k_ref, v_ref)):
        cols = slice(j * 256, (j + 1) * 256)
        o_ref[:, cols] = dot(x_ref[...], ref[...], TN) + r_ref[:, cols]


def local_part(at, x, loc, arrived, name):
    mine = arrived is not None

    def cols(first):
        return pl.BlockSpec((TOK, 256), lambda i, s: (0, first + (s[0] if mine else 1 - s[0])))

    rows = pl.BlockSpec((DM // 2, 768), lambda i, s: (i, 0))
    return pl.pallas_call(
        keep_body if mine else give_body,
        grid_spec=pltpu.PrefetchScalarGridSpec(
            num_scalar_prefetch=1,
            grid=(2,),
            in_specs=[pl.BlockSpec((TOK, DM // 2), lambda i, s: (0, i)), cols(0), cols(2), cols(4)]
            + ([rows] if mine else []),
            out_specs=rows,
        ),
        out_shape=jax.ShapeDtypeStruct((DM, 768), F32),
        compiler_params=params(24),
        cost_estimate=cost(3e9, 12e6),
        name=name,
    )(at, x, loc, loc, loc, *([arrived] if mine else []))


def pick(at_ref, axis):
    mine, far, first, second = (at_ref[1 + 4 * axis + i] for i in range(4))
    return (mine, second), (first, far)


def finish_body(at_ref, w_ref, a_ref, b_ref, sa_ref, sb_ref, kx_ref, sx_ref, ky_ref, sy_ref, s_ref):
    j = pl.program_id(0)
    core = at_ref[0]

    def add(kind, dims):
        for i in range(2):
            cols = slice(i * HD, (i + 1) * HD)
            h = 2 * core + i
            term = dot(a_ref[:, cols], sa_ref[kind, h].astype(BF16), dims)
            term += dot(b_ref[:, cols].astype(BF16), sb_ref[kind, h].astype(BF16), dims)
            s_ref[:, :, :, :, cols] = (w_ref[:, cols] + term).reshape(8, 4, 4, 8, HD)

    @pl.when(j == 0)
    def _():
        add(0, NT)

    @pl.when(j == 1)
    def _():
        add(1, NT)

    @pl.when(j == 2)
    def _():
        add(1, NN)

    kept, sent = pick(at_ref, 0)
    for i in range(2):
        kx_ref[:, :, i] = s_ref[:, :, kept[i], :, 0:128]
        sx_ref[:, :, i] = s_ref[:, :, sent[i], :, 0:128]
    kept, sent = pick(at_ref, 1)
    for i in range(2):
        ky_ref[:, i] = s_ref[:, kept[i], :, :, 128:256]
        sy_ref[:, i] = s_ref[:, sent[i], :, :, 128:256]


def finish(at, w, a, b, sa, sb):
    bx = pl.BlockSpec((8, 4, 2, 8, 128), lambda j, s: (0, 0, 0, 0, j))
    by = pl.BlockSpec((8, 2, 4, 8, 128), lambda j, s: (0, 0, 0, 0, j))
    cols = pl.BlockSpec((DM, 256), lambda j, s: (0, j))
    states = pl.BlockSpec((2, H, HD, HD), lambda j, s: (0, 0, 0, 0))
    return pl.pallas_call(
        finish_body,
        grid_spec=pltpu.PrefetchScalarGridSpec(
            num_scalar_prefetch=1,
            grid=(3,),
            in_specs=[cols, cols, cols, states, states],
            out_specs=[bx, bx, by, by],
            scratch_shapes=[pltpu.VMEM((8, 4, 4, 8, 256), F32)],
        ),
        out_shape=[jax.ShapeDtypeStruct((8, 4, 2, 8, 384), F32)] * 2
        + [jax.ShapeDtypeStruct((8, 2, 4, 8, 384), F32)] * 2,
        compiler_params=params(24),
        cost_estimate=cost(1e9, 12e6),
        name="finish",
    )(at, w, a, b, sa, sb)


def inputs_body(loc_ref, qkv_ref, sg_ref, s_ref, w_ref, o_ref, d_ref):
    for h in range(H):
        before = s_ref[0, h].astype(BF16)
        after = s_ref[1, h].astype(BF16)
        parts = (
            dot(sg_ref[:, pl.ds(h * HD, HD)], before, NT),
            dot(qkv_ref[:, head(2, h)], after, NT),
            dot(qkv_ref[:, head(1, h)], after, NN),
        )
        for p, d in enumerate(parts):
            d_ref[:, head(p, h)] = (loc_ref[:, head(p, h)].astype(F32) + d).astype(BF16)
    o_ref[...] = dot(d_ref[...], w_ref[...], NT).astype(BF16)


def inputs_grad(loc, qkv, sg, states, weights):
    block = lambda cols: pl.BlockSpec((CH, cols), lambda n: (n, 0))
    return pl.pallas_call(
        inputs_body,
        grid=(NB,),
        in_specs=[
            block(3 * D),
            block(3 * D),
            block(D),
            pl.BlockSpec((2, H, HD, HD), lambda n: (0, 0, 0, 0)),
            pl.BlockSpec((DM, 3 * D), lambda n: (0, 0)),
        ],
        out_specs=block(DM),
        out_shape=jax.ShapeDtypeStruct((TOK, DM), BF16),
        scratch_shapes=[pltpu.VMEM((CH, 3 * D), BF16)],
        compiler_params=params(24),
        cost_estimate=cost(5e9, 14e6),
        name="inputs_grad",
    )(loc, qkv, sg, states, weights)


def whole_call(body, name, shapes, *args, scratch=()):
    vmem = pl.BlockSpec(memory_space=pltpu.VMEM)
    smem = pl.BlockSpec(memory_space=pltpu.SMEM)
    return pl.pallas_call(
        body,
        in_specs=[smem if a.dtype == jnp.int32 else vmem for a in args],
        out_specs=[vmem] * len(shapes),
        out_shape=[jax.ShapeDtypeStruct(s, F32) for s in shapes],
        scratch_shapes=list(scratch),
        compiler_params=params(16),
        name=name,
    )(*args)


def add1_body(kx, rx, ky, ry, kx2, sx2, ky2, sy2):
    kx2[...] = kx[:, :, 0] + rx[:, :, 0]
    sx2[...] = kx[:, :, 1] + rx[:, :, 1]
    ky2[...] = ky[:, 0] + ry[:, 0]
    sy2[...] = ky[:, 1] + ry[:, 1]


def add2_body(at, kx, rx, ky, ry, kp, sp, kq, sq):
    for axis, k, r, ko, so in ((1, kx, rx, kp, sp), (0, ky, ry, kq, sq)):
        kept, sent = pick(at, axis)
        for i in range(2):
            ko[:, i] = k[:, kept[i]] + r[:, kept[i]]
            so[:, i] = k[:, sent[i]] + r[:, sent[i]]


def add3_body(kp, rp, kq, rq, kp2, sp2, kq2, sq2):
    for k, r, ko, so in ((kp, rp, kp2, sp2), (kq, rq, kq2, sq2)):
        ko[...] = k[:, 0] + r[:, 0]
        so[...] = k[:, 1] + r[:, 1]


def add4_body(kp, rp, kq, rq, o):
    o[:, :, 0:384] = kp[...] + rp[...]
    o[:, :, 384:768] = kq[...] + rq[...]


def sum_body(v, o):
    total = v[0]
    for i in range(1, v.shape[0]):
        total = total + v[i]
    for i in range(o.shape[0]):
        o[i] = total


def place_body(v, o):
    for i in range(8):
        for p in range(6):
            at = (p % 3) * 512 + (i % 2) * 256 + (p // 3) * 128
            o[i // 2 * 8 : i // 2 * 8 + 8, at : at + 128] = v[i, :, p * 128 : (p + 1) * 128]


def exchange(value, axis, step):
    pairs = []
    for i in range(4):
        for c in range(2):
            j = i ^ ((1, 3), (3, 1))[c][step]
            pairs.append((2 * i + c, 2 * j + c))
    return lax.ppermute(value, (axis, "core"), pairs)


def shards(inputs, weights, out_grad):
    x = inputs[0]
    z_at, y_at, x_at, core = (lax.axis_index(a) for a in ("z", "y", "x", "core"))
    tm_at = z_at * 4 + y_at
    first = jnp.where(core == 0, 1, 3)
    second = 4 - first
    at = jnp.stack(
        [core]
        + [v for i in (x_at, y_at) for v in (i, i ^ first ^ second, i ^ first, i ^ second)]
    ).astype(jnp.int32)
    offset = (tm_at * TOK).astype(jnp.int32)[None]
    back = (tm_at >= 16).astype(jnp.int32)[None]

    qkv, sg, kv, qg, total = project(offset, x, weights, out_grad[0])
    slices = lax.all_to_all(total.reshape(32, 32, HD), ("z", "y"), 0, 0, tiled=True)
    factors_out = factors(at, x, sg, qkv, False, F32, "factors_give")
    loc = local(qkv, sg, kv, qg)
    local_out = local_part(at, x, loc, None, "local_give")
    slices, factors_out, local_out = lax.optimization_barrier((slices, factors_out, local_out))
    factors_in = lax.ppermute(factors_out, "core", SWAP)
    local_in = lax.ppermute(local_out, "core", SWAP)

    scanned = scan_states(back, slices, [])
    states = lax.all_to_all(scanned, ("z", "y"), 0, 0, tiled=True)
    mine = factors(at, x, sg, qkv, True, BF16, "factors_keep")
    both = local_part(at, x, loc, local_in, "local_keep")
    states, mine, both = lax.optimization_barrier((states, mine, both))

    states = states.reshape(2, H, HD, HD)
    states_in = lax.ppermute(states, "core", SWAP)
    kx, sx, ky, sy = finish(at, both, mine, factors_in, states, states_in)
    rx = exchange(sx, "x", 0)
    ry = exchange(sy, "y", 0)
    record_grad = inputs_grad(loc, qkv, sg, states, weights)
    kx, sx, ky, sy = whole_call(add1_body, "add1", [(8, 4, 8, 384)] * 4, kx, rx, ky, ry)
    rx = exchange(sx, "x", 1)
    ry = exchange(sy, "y", 1)
    kp, sp, kq, sq = whole_call(add2_body, "add2", [(8, 2, 8, 384)] * 4, at, kx, rx, ky, ry)
    rp = exchange(sp, "y", 0)
    rq = exchange(sq, "x", 0)
    kp, sp, kq, sq = whole_call(add3_body, "add3", [(8, 8, 384)] * 4, kp, rp, kq, rq)
    rp = exchange(sp, "y", 1)
    rq = exchange(sq, "x", 1)
    (part,) = whole_call(add4_body, "add4", [(8, 8, 768)], kp, rp, kq, rq)
    part = lax.all_to_all(part, "z", 0, 0, tiled=True)
    (mine,) = whole_call(sum_body, "sum_z", [(8, 8, 768)], part)
    rows = lax.all_to_all(mine, ("x", "core"), 0, 0, tiled=True)
    (proj_grad,) = whole_call(place_body, "place", [(32, 3 * D)], rows)
    return record_grad[None], proj_grad


def solution(mesh):
    fine = Mesh(mesh.devices.reshape(8, 4, 4, 2), ("z", "y", "x", "core"))
    tm, dp = ("z", "y"), ("x", "core")
    placed = (P(dp, tm, None), P(), P(dp, tm, None))
    return jax.shard_map(
        shards,
        mesh=fine,
        in_specs=placed,
        out_specs=(P(dp, tm, None), P(tm, None)),
        check_vma=False,
    )
```

```python
import functools

import jax
import jax.numpy as jnp
from jax import lax
from jax.experimental import pallas as pl
from jax.experimental.pallas import tpu as pltpu
from jax.sharding import Mesh, PartitionSpec as P

H = 4
HD = 128
CH = 256
NB = 4
D = H * HD
DM = 1024
TOK = NB * CH
F32 = jnp.float32
BF16 = jnp.bfloat16

NN = (((1,), (0,)), ((), ()))
NT = (((1,), (1,)), ((), ()))
TN = (((0,), (0,)), ((), ()))


def dot(a, b, dims):
    return lax.dot_general(a, b, dims, preferred_element_type=F32)


MIB = 1024 * 1024
SWAP = [(0, 1), (1, 0)]


def params(mib=40):
    return pltpu.CompilerParams(vmem_limit_bytes=mib * MIB)


def cost(flops, moved):
    return pl.CostEstimate(flops=int(flops), bytes_accessed=int(moved), transcendentals=0)


def head(part, h):
    return pl.ds(part * D + h * HD, HD)


def project_body(pos_ref, x_ref, w_ref, g_ref, qkv_ref, sg_ref, kv_ref, qg_ref, total_ref):
    n = pl.program_id(0)
    qkv_ref[...] = dot(x_ref[...], w_ref[...], NN).astype(BF16)
    pos = (pos_ref[0] + n * CH + lax.broadcasted_iota(jnp.int32, (CH, 1), 0)).astype(F32)
    factor = 1.0 / jnp.sqrt(jnp.float32(HD) * (pos + 1.0))
    sg_ref[...] = (g_ref[...].astype(F32) * factor).astype(BF16)

    @pl.when(n == 0)
    def _():
        total_ref[...] = jnp.zeros_like(total_ref)

    for h in range(H):
        kv = dot(qkv_ref[:, head(1, h)], qkv_ref[:, head(2, h)], TN)
        qg = dot(qkv_ref[:, head(0, h)], sg_ref[:, pl.ds(h * HD, HD)], TN)
        kv_ref[0, h] = kv
        qg_ref[0, h] = qg
        total_ref[0, h] += kv
        total_ref[1, h] += qg


def project(offset, x, w, g):
    block = lambda cols: pl.BlockSpec((CH, cols), lambda n, s: (n, 0))
    sums = pl.BlockSpec((1, H, HD, HD), lambda n, s: (n, 0, 0, 0))
    return pl.pallas_call(
        project_body,
        grid_spec=pltpu.PrefetchScalarGridSpec(
            num_scalar_prefetch=1,
            grid=(NB,),
            in_specs=[block(DM), pl.BlockSpec((DM, 3 * D), lambda n, s: (0, 0)), block(D)],
            out_specs=[
                block(3 * D),
                block(D),
                sums,
                sums,
                pl.BlockSpec((2, H, HD, HD), lambda n, s: (0, 0, 0, 0)),
            ],
        ),
        out_shape=[
            jax.ShapeDtypeStruct((TOK, 3 * D), BF16),
            jax.ShapeDtypeStruct((TOK, D), BF16),
            jax.ShapeDtypeStruct((NB, H, HD, HD), F32),
            jax.ShapeDtypeStruct((NB, H, HD, HD), F32),
            jax.ShapeDtypeStruct((2, H, HD, HD), F32),
        ],
        compiler_params=params(60),
        name="project",
    )(offset, x, w, g)


def scan_body(count, back_ref, v_ref, o_ref):

    def step(t, so_far):
        i = jnp.where(back_ref[0] == 1, count - 1 - t, t)
        o_ref[i] = so_far
        return so_far + v_ref[i]

    lax.fori_loop(0, count, step, jnp.zeros(v_ref.shape[1:], F32))


def scan_states(back, v):
    return pl.pallas_call(
        functools.partial(scan_body, v.shape[0]),
        in_specs=[pl.BlockSpec(memory_space=pltpu.SMEM), pl.BlockSpec(memory_space=pltpu.VMEM)],
        out_specs=pl.BlockSpec(memory_space=pltpu.VMEM),
        out_shape=jax.ShapeDtypeStruct(v.shape, F32),
        compiler_params=params(4),
        name="scan_states",
    )(back, v)


def local_body(qkv_ref, sg_ref, kv_ref, qg_ref, o_ref):
    n = pl.program_id(0)
    keep = lax.broadcasted_iota(jnp.int32, (CH, CH), 0) >= lax.broadcasted_iota(jnp.int32, (CH, CH), 1)
    for h in range(H):
        q, k, v = (qkv_ref[:, head(p, h)] for p in range(3))
        g = sg_ref[:, pl.ds(h * HD, HD)]
        before = jnp.zeros((HD, HD), F32)
        after = jnp.zeros((HD, HD), F32)
        for m in range(NB):
            before = before + jnp.where(m < n, kv_ref[m, h], 0.0)
            after = after + jnp.where(m > n, qg_ref[m, h], 0.0)
        before = before.astype(BF16)
        after = after.astype(BF16)
        mvg = jnp.where(keep, dot(g, v, NT), 0.0).astype(BF16)
        mqk = jnp.where(keep, dot(q, k, NT), 0.0).astype(BF16)
        dq = dot(mvg, k, NN) + dot(g, before, NT)
        dk = dot(mvg, q, TN) + dot(v, after, NT)
        dv = dot(mqk, g, TN) + dot(k, after, NN)
        for p, d in enumerate((dq, dk, dv)):
            o_ref[:, head(p, h)] = d.astype(BF16)


def local(qkv, sg, kv, qg):
    block = lambda cols: pl.BlockSpec((CH, cols), lambda n: (n, 0))
    sums = pl.BlockSpec((NB, H, HD, HD), lambda n: (0, 0, 0, 0))
    return pl.pallas_call(
        local_body,
        grid=(NB,),
        in_specs=[block(3 * D), block(D), sums, sums],
        out_specs=block(3 * D),
        out_shape=jax.ShapeDtypeStruct((TOK, 3 * D), BF16),
        compiler_params=params(20),
        cost_estimate=cost(4e9, 20e6),
        name="local",
    )(qkv, sg, kv, qg)


def factors_body(at_ref, x_ref, g_ref, k_ref, v_ref, o_ref):
    for j, ref in enumerate((g_ref, v_ref, k_ref)):
        o_ref[:, j * 256 : (j + 1) * 256] = dot(x_ref[...], ref[...], TN).astype(o_ref.dtype)


def factors(at, x, sg, qkv, mine, kind, name):
    def cols(first):
        return pl.BlockSpec((TOK, 256), lambda i, s: (0, first + (s[0] if mine else 1 - s[0])))

    return pl.pallas_call(
        factors_body,
        grid_spec=pltpu.PrefetchScalarGridSpec(
            num_scalar_prefetch=1,
            grid=(2,),
            in_specs=[pl.BlockSpec((TOK, DM // 2), lambda i, s: (0, i)), cols(0), cols(2), cols(4)],
            out_specs=pl.BlockSpec((DM // 2, 768), lambda i, s: (i, 0)),
        ),
        out_shape=jax.ShapeDtypeStruct((DM, 768), kind),
        compiler_params=params(24),
        cost_estimate=cost(3e9, 12e6),
        name=name,
    )(at, x, sg, qkv, qkv)


def give_body(at_ref, x_ref, q_ref, k_ref, v_ref, o_ref):
    for j, ref in enumerate((q_ref, k_ref, v_ref)):
        o_ref[:, j * 256 : (j + 1) * 256] = dot(x_ref[...], ref[...], TN)


def keep_body(at_ref, x_ref, q_ref, k_ref, v_ref, r_ref, o_ref):
    for j, ref in enumerate((q_ref, k_ref, v_ref)):
        cols = slice(j * 256, (j + 1) * 256)
        o_ref[:, cols] = dot(x_ref[...], ref[...], TN) + r_ref[:, cols]


def local_part(at, x, loc, arrived, name):
    mine = arrived is not None

    def cols(first):
        return pl.BlockSpec((TOK, 256), lambda i, s: (0, first + (s[0] if mine else 1 - s[0])))

    rows = pl.BlockSpec((DM // 2, 768), lambda i, s: (i, 0))
    return pl.pallas_call(
        keep_body if mine else give_body,
        grid_spec=pltpu.PrefetchScalarGridSpec(
            num_scalar_prefetch=1,
            grid=(2,),
            in_specs=[pl.BlockSpec((TOK, DM // 2), lambda i, s: (0, i)), cols(0), cols(2), cols(4)]
            + ([rows] if mine else []),
            out_specs=rows,
        ),
        out_shape=jax.ShapeDtypeStruct((DM, 768), F32),
        compiler_params=params(24),
        cost_estimate=cost(3e9, 12e6),
        name=name,
    )(at, x, loc, loc, loc, *([arrived] if mine else []))


def pick(at_ref, axis):
    mine, far, first, second = (at_ref[1 + 4 * axis + i] for i in range(4))
    return (mine, second), (first, far)


def finish_body(at_ref, w_hbm, a_hbm, b_hbm, sa_ref, sb_ref, kx_ref, sx_ref, ky_ref, sy_ref, w_ref, a_ref, b_ref, s_ref, sems):
    core = at_ref[0]
    copies = []
    for j in range(3):
        cols = pl.ds(j * 256, 256)
        copies.append(
            (
                pltpu.make_async_copy(w_hbm.at[:, cols], w_ref.at[j], sems.at[0, j]),
                pltpu.make_async_copy(a_hbm.at[:, cols], a_ref.at[j], sems.at[1, j]),
                pltpu.make_async_copy(b_hbm.at[:, cols], b_ref.at[j], sems.at[2, j]),
            )
        )
    for pair in copies:
        for copy in pair:
            copy.start()
    for j, (kind, dims) in enumerate(((0, NT), (1, NT), (1, NN))):
        for copy in copies[j]:
            copy.wait()
        for i in range(2):
            cols = slice(i * HD, (i + 1) * HD)
            h = 2 * core + i
            far = b_ref[j, :, cols].astype(BF16)
            term = dot(a_ref[j, :, cols], sa_ref[kind, h].astype(BF16), dims)
            term += dot(far, sb_ref[kind, h].astype(BF16), dims)
            s_ref[j, :, :, :, :, cols] = (w_ref[j, :, cols] + term).reshape(8, 4, 4, 8, HD)
        lanes = slice(j * HD, (j + 1) * HD)
        kept, sent = pick(at_ref, 0)
        for i in range(2):
            kx_ref[:, :, i, :, lanes] = s_ref[j, :, :, kept[i], :, 0:128]
            sx_ref[:, :, i, :, lanes] = s_ref[j, :, :, sent[i], :, 0:128]
        kept, sent = pick(at_ref, 1)
        for i in range(2):
            ky_ref[:, i, :, :, lanes] = s_ref[j, :, kept[i], :, :, 128:256]
            sy_ref[:, i, :, :, lanes] = s_ref[j, :, sent[i], :, :, 128:256]


def finish(at, w, a, b, sa, sb):
    vmem = pl.BlockSpec(memory_space=pltpu.VMEM)
    hbm = pl.BlockSpec(memory_space=pltpu.HBM)
    return pl.pallas_call(
        finish_body,
        in_specs=[pl.BlockSpec(memory_space=pltpu.SMEM), hbm, hbm, hbm, vmem, vmem],
        out_specs=[vmem] * 4,
        out_shape=[jax.ShapeDtypeStruct((8, 4, 2, 8, 384), F32)] * 2
        + [jax.ShapeDtypeStruct((8, 2, 4, 8, 384), F32)] * 2,
        scratch_shapes=[
            pltpu.VMEM((3, DM, 256), F32),
            pltpu.VMEM((3, DM, 256), BF16),
            pltpu.VMEM((3, DM, 256), F32),
            pltpu.VMEM((3, 8, 4, 4, 8, 256), F32),
            pltpu.SemaphoreType.DMA((3, 3)),
        ],
        compiler_params=params(49),
        cost_estimate=cost(1e9, 12e6),
        name="finish",
    )(at, w, a, b, sa, sb)


def inputs_body(loc_ref, qkv_ref, sg_ref, s_ref, w_ref, o_ref, d_ref):
    for h in range(H):
        before = s_ref[0, h].astype(BF16)
        after = s_ref[1, h].astype(BF16)
        parts = (
            dot(sg_ref[:, pl.ds(h * HD, HD)], before, NT),
            dot(qkv_ref[:, head(2, h)], after, NT),
            dot(qkv_ref[:, head(1, h)], after, NN),
        )
        for p, d in enumerate(parts):
            d_ref[:, head(p, h)] = (loc_ref[:, head(p, h)].astype(F32) + d).astype(BF16)
    o_ref[...] = dot(d_ref[...], w_ref[...], NT).astype(BF16)


def inputs_grad(loc, qkv, sg, states, weights):
    block = lambda cols: pl.BlockSpec((CH, cols), lambda n: (n, 0))
    return pl.pallas_call(
        inputs_body,
        grid=(NB,),
        in_specs=[
            block(3 * D),
            block(3 * D),
            block(D),
            pl.BlockSpec((2, H, HD, HD), lambda n: (0, 0, 0, 0)),
            pl.BlockSpec((DM, 3 * D), lambda n: (0, 0)),
        ],
        out_specs=block(DM),
        out_shape=jax.ShapeDtypeStruct((TOK, DM), BF16),
        scratch_shapes=[pltpu.VMEM((CH, 3 * D), BF16)],
        compiler_params=params(48),
        cost_estimate=cost(5e9, 14e6),
        name="inputs_grad",
    )(loc, qkv, sg, states, weights)


def whole_call(body, name, shapes, *args, scratch=()):
    vmem = pl.BlockSpec(memory_space=pltpu.VMEM)
    smem = pl.BlockSpec(memory_space=pltpu.SMEM)
    return pl.pallas_call(
        body,
        in_specs=[smem if a.dtype == jnp.int32 else vmem for a in args],
        out_specs=[vmem] * len(shapes),
        out_shape=[jax.ShapeDtypeStruct(s, F32) for s in shapes],
        scratch_shapes=list(scratch),
        compiler_params=params(16),
        name=name,
    )(*args)


def add1_body(kx, rx, ky, ry, kx2, sx2, ky2, sy2):
    kx2[...] = kx[:, :, 0] + rx[:, :, 0]
    sx2[...] = kx[:, :, 1] + rx[:, :, 1]
    ky2[...] = ky[:, 0] + ry[:, 0]
    sy2[...] = ky[:, 1] + ry[:, 1]


def add2_body(at, kx, rx, ky, ry, kp, sp, kq, sq):
    for axis, k, r, ko, so in ((1, kx, rx, kp, sp), (0, ky, ry, kq, sq)):
        kept, sent = pick(at, axis)
        for i in range(2):
            ko[:, i] = k[:, kept[i]] + r[:, kept[i]]
            so[:, i] = k[:, sent[i]] + r[:, sent[i]]


def add3_body(kp, rp, kq, rq, kp2, sp2, kq2, sq2):
    for k, r, ko, so in ((kp, rp, kp2, sp2), (kq, rq, kq2, sq2)):
        ko[...] = k[:, 0] + r[:, 0]
        so[...] = k[:, 1] + r[:, 1]


def add4_body(kp, rp, kq, rq, o):
    o[:, :, 0:384] = kp[...] + rp[...]
    o[:, :, 384:768] = kq[...] + rq[...]


def sum_body(v, o):
    total = v[0]
    for i in range(1, v.shape[0]):
        total = total + v[i]
    for i in range(o.shape[0]):
        o[i] = total


def place_body(v, o):
    for i in range(8):
        for p in range(6):
            at = (p % 3) * 512 + (i % 2) * 256 + (p // 3) * 128
            o[i // 2 * 8 : i // 2 * 8 + 8, at : at + 128] = v[i, :, p * 128 : (p + 1) * 128]


def exchange(value, axis, step):
    pairs = []
    for i in range(4):
        for c in range(2):
            j = i ^ ((1, 3), (3, 1))[c][step]
            pairs.append((2 * i + c, 2 * j + c))
    return lax.ppermute(value, (axis, "core"), pairs)


def shards(inputs, weights, out_grad):
    x = inputs[0]
    z_at, y_at, x_at, core = (lax.axis_index(a) for a in ("z", "y", "x", "core"))
    tm_at = z_at * 4 + y_at
    first = jnp.where(core == 0, 1, 3)
    second = 4 - first
    at = jnp.stack(
        [core]
        + [v for i in (x_at, y_at) for v in (i, i ^ first ^ second, i ^ first, i ^ second)]
    ).astype(jnp.int32)
    offset = (tm_at * TOK).astype(jnp.int32)[None]
    back = (tm_at >= 16).astype(jnp.int32)[None]

    qkv, sg, kv, qg, total = project(offset, x, weights, out_grad[0])
    slices = lax.all_to_all(total.reshape(32, 32, HD), ("z", "y"), 0, 0, tiled=True)
    factors_out = factors(at, x, sg, qkv, False, F32, "factors_give")
    loc = local(qkv, sg, kv, qg)
    local_out = local_part(at, x, loc, None, "local_give")
    slices, factors_out, local_out = lax.optimization_barrier((slices, factors_out, local_out))
    factors_in = lax.ppermute(factors_out, "core", SWAP)
    local_in = lax.ppermute(local_out, "core", SWAP)

    scanned = scan_states(back, slices)
    states = lax.all_to_all(scanned, ("z", "y"), 0, 0, tiled=True)
    mine = factors(at, x, sg, qkv, True, BF16, "factors_keep")
    both = local_part(at, x, loc, local_in, "local_keep")
    states, mine, both = lax.optimization_barrier((states, mine, both))

    states = states.reshape(2, H, HD, HD)
    states_in = lax.ppermute(states, "core", SWAP)
    kx, sx, ky, sy = finish(at, both, mine, factors_in, states, states_in)
    rx = exchange(sx, "x", 0)
    ry = exchange(sy, "y", 0)
    record_grad = inputs_grad(loc, qkv, sg, states, weights)
    rx, ry, record_grad = lax.optimization_barrier((rx, ry, record_grad))
    kx, sx, ky, sy = whole_call(add1_body, "add1", [(8, 4, 8, 384)] * 4, kx, rx, ky, ry)
    rx = exchange(sx, "x", 1)
    ry = exchange(sy, "y", 1)
    kp, sp, kq, sq = whole_call(add2_body, "add2", [(8, 2, 8, 384)] * 4, at, kx, rx, ky, ry)
    rp = exchange(sp, "y", 0)
    rq = exchange(sq, "x", 0)
    kp, sp, kq, sq = whole_call(add3_body, "add3", [(8, 8, 384)] * 4, kp, rp, kq, rq)
    rp = exchange(sp, "y", 1)
    rq = exchange(sq, "x", 1)
    (part,) = whole_call(add4_body, "add4", [(8, 8, 768)], kp, rp, kq, rq)
    part = lax.all_to_all(part, "z", 0, 0, tiled=True)
    (mine,) = whole_call(sum_body, "sum_z", [(8, 8, 768)], part)
    rows = lax.all_to_all(mine, ("x", "core"), 0, 0, tiled=True)
    (proj_grad,) = whole_call(place_body, "place", [(32, 3 * D)], rows)
    return record_grad[None], proj_grad


def solution(mesh):
    fine = Mesh(mesh.devices.reshape(8, 4, 4, 2), ("z", "y", "x", "core"))
    tm, dp = ("z", "y"), ("x", "core")
    placed = (P(dp, tm, None), P(), P(dp, tm, None))
    return jax.shard_map(
        shards,
        mesh=fine,
        in_specs=placed,
        out_specs=(P(dp, tm, None), P(tm, None)),
        check_vma=False,
    )
```

```python
import functools

import jax
import jax.numpy as jnp
from jax import lax
from jax.experimental import pallas as pl
from jax.experimental.pallas import tpu as pltpu
from jax.sharding import Mesh, PartitionSpec as P

H = 4
HD = 128
CH = 256
NB = 4
D = H * HD
DM = 1024
TOK = NB * CH
F32 = jnp.float32
BF16 = jnp.bfloat16

NN = (((1,), (0,)), ((), ()))
NT = (((1,), (1,)), ((), ()))
TN = (((0,), (0,)), ((), ()))


def dot(a, b, dims):
    return lax.dot_general(a, b, dims, preferred_element_type=F32)


MIB = 1024 * 1024
SWAP = [(0, 1), (1, 0)]


def params(mib=40):
    return pltpu.CompilerParams(vmem_limit_bytes=mib * MIB)


def cost(flops, moved):
    return pl.CostEstimate(flops=int(flops), bytes_accessed=int(moved), transcendentals=0)


def head(part, h):
    return pl.ds(part * D + h * HD, HD)


def project_body(pos_ref, x_ref, w_ref, g_ref, qkv_ref, sg_ref, kv_ref, qg_ref, total_ref):
    n = pl.program_id(0)
    qkv_ref[...] = dot(x_ref[...], w_ref[...], NN).astype(BF16)
    pos = (pos_ref[0] + n * CH + lax.broadcasted_iota(jnp.int32, (CH, 1), 0)).astype(F32)
    factor = 1.0 / jnp.sqrt(jnp.float32(HD) * (pos + 1.0))
    sg_ref[...] = (g_ref[...].astype(F32) * factor).astype(BF16)

    @pl.when(n == 0)
    def _():
        total_ref[...] = jnp.zeros_like(total_ref)

    for h in range(H):
        kv = dot(qkv_ref[:, head(1, h)], qkv_ref[:, head(2, h)], TN)
        qg = dot(qkv_ref[:, head(0, h)], sg_ref[:, pl.ds(h * HD, HD)], TN)
        kv_ref[0, h] = kv
        qg_ref[0, h] = qg
        total_ref[0, h] += kv
        total_ref[1, h] += qg


def project(offset, x, w, g):
    block = lambda cols: pl.BlockSpec((CH, cols), lambda n, s: (n, 0))
    sums = pl.BlockSpec((1, H, HD, HD), lambda n, s: (n, 0, 0, 0))
    return pl.pallas_call(
        project_body,
        grid_spec=pltpu.PrefetchScalarGridSpec(
            num_scalar_prefetch=1,
            grid=(NB,),
            in_specs=[block(DM), pl.BlockSpec((DM, 3 * D), lambda n, s: (0, 0)), block(D)],
            out_specs=[
                block(3 * D),
                block(D),
                sums,
                sums,
                pl.BlockSpec((2, H, HD, HD), lambda n, s: (0, 0, 0, 0)),
            ],
        ),
        out_shape=[
            jax.ShapeDtypeStruct((TOK, 3 * D), BF16),
            jax.ShapeDtypeStruct((TOK, D), BF16),
            jax.ShapeDtypeStruct((NB, H, HD, HD), F32),
            jax.ShapeDtypeStruct((NB, H, HD, HD), F32),
            jax.ShapeDtypeStruct((2, H, HD, HD), F32),
        ],
        compiler_params=params(60),
        name="project",
    )(offset, x, w, g)


def scan_body(count, back_ref, v_ref, o_ref):

    def step(t, so_far):
        i = jnp.where(back_ref[0] == 1, count - 1 - t, t)
        o_ref[i] = so_far
        return so_far + v_ref[i]

    lax.fori_loop(0, count, step, jnp.zeros(v_ref.shape[1:], F32))


def scan_states(back, v):
    return pl.pallas_call(
        functools.partial(scan_body, v.shape[0]),
        in_specs=[pl.BlockSpec(memory_space=pltpu.SMEM), pl.BlockSpec(memory_space=pltpu.VMEM)],
        out_specs=pl.BlockSpec(memory_space=pltpu.VMEM),
        out_shape=jax.ShapeDtypeStruct(v.shape, F32),
        compiler_params=params(4),
        name="scan_states",
    )(back, v)


def local_body(qkv_ref, sg_ref, kv_ref, qg_ref, o_ref):
    n = pl.program_id(0)
    keep = lax.broadcasted_iota(jnp.int32, (CH, CH), 0) >= lax.broadcasted_iota(jnp.int32, (CH, CH), 1)
    for h in range(H):
        q, k, v = (qkv_ref[:, head(p, h)] for p in range(3))
        g = sg_ref[:, pl.ds(h * HD, HD)]
        before = jnp.zeros((HD, HD), F32)
        after = jnp.zeros((HD, HD), F32)
        for m in range(NB):
            before = before + jnp.where(m < n, kv_ref[m, h], 0.0)
            after = after + jnp.where(m > n, qg_ref[m, h], 0.0)
        before = before.astype(BF16)
        after = after.astype(BF16)
        mvg = jnp.where(keep, dot(g, v, NT), 0.0).astype(BF16)
        mqk = jnp.where(keep, dot(q, k, NT), 0.0).astype(BF16)
        dq = dot(mvg, k, NN) + dot(g, before, NT)
        dk = dot(mvg, q, TN) + dot(v, after, NT)
        dv = dot(mqk, g, TN) + dot(k, after, NN)
        for p, d in enumerate((dq, dk, dv)):
            o_ref[:, head(p, h)] = d.astype(BF16)


def local(qkv, sg, kv, qg):
    block = lambda cols: pl.BlockSpec((CH, cols), lambda n: (n, 0))
    sums = pl.BlockSpec((NB, H, HD, HD), lambda n: (0, 0, 0, 0))
    return pl.pallas_call(
        local_body,
        grid=(NB,),
        in_specs=[block(3 * D), block(D), sums, sums],
        out_specs=block(3 * D),
        out_shape=jax.ShapeDtypeStruct((TOK, 3 * D), BF16),
        compiler_params=params(60),
        cost_estimate=cost(4e9, 20e6),
        name="local",
    )(qkv, sg, kv, qg)


def give_body(at_ref, x_ref, *refs):
    for j, ref in enumerate(refs[:3]):
        refs[3][:, j * 256 : (j + 1) * 256] = dot(x_ref[...], ref[...], TN)


def give(at, x, sources, name):
    cols = [pl.BlockSpec((TOK, 256), lambda i, s, f=f: (0, f + 1 - s[0])) for _, f in sources]
    return pl.pallas_call(
        give_body,
        grid_spec=pltpu.PrefetchScalarGridSpec(
            num_scalar_prefetch=1,
            grid=(4,),
            in_specs=[pl.BlockSpec((TOK, DM // 4), lambda i, s: (0, i))] + cols,
            out_specs=pl.BlockSpec((DM // 4, 768), lambda i, s: (i, 0)),
        ),
        out_shape=jax.ShapeDtypeStruct((DM, 768), F32),
        compiler_params=params(60),
        cost_estimate=cost(3e9, 12e6),
        name=name,
    )(at, x, *(a for a, _ in sources))


def keep_body(at_ref, x_ref, r_ref, *refs):
    w_ref, f_ref = refs[6:]
    for j in range(3):
        cols = slice(j * 256, (j + 1) * 256)
        w_ref[:, cols] = dot(x_ref[...], refs[j][...], TN) + r_ref[:, cols]
        f_ref[:, cols] = dot(x_ref[...], refs[3 + j][...], TN).astype(BF16)


def keep(at, x, arrived, sources):
    cols = [pl.BlockSpec((TOK, 256), lambda i, s, f=f: (0, f + s[0])) for _, f in sources]
    rows = pl.BlockSpec((DM // 4, 768), lambda i, s: (i, 0))
    return pl.pallas_call(
        keep_body,
        grid_spec=pltpu.PrefetchScalarGridSpec(
            num_scalar_prefetch=1,
            grid=(4,),
            in_specs=[pl.BlockSpec((TOK, DM // 4), lambda i, s: (0, i)), rows] + cols,
            out_specs=[rows, rows],
        ),
        out_shape=[jax.ShapeDtypeStruct((DM, 768), F32), jax.ShapeDtypeStruct((DM, 768), BF16)],
        compiler_params=params(60),
        cost_estimate=cost(40e9, 16e6),
        name="keep",
    )(at, x, arrived, *(a for a, _ in sources))


def pick(at_ref, axis):
    mine, far, first, second = (at_ref[1 + 4 * axis + i] for i in range(4))
    return (mine, second), (first, far)


def finish_body(at_ref, w_hbm, a_hbm, b_hbm, sa_ref, sb_ref, kx_ref, sx_ref, ky_ref, sy_ref, w_ref, a_ref, b_ref, s_ref, sems):
    core = at_ref[0]
    copies = []
    for j in range(3):
        cols = pl.ds(j * 256, 256)
        copies.append(
            (
                pltpu.make_async_copy(w_hbm.at[:, cols], w_ref.at[j], sems.at[0, j]),
                pltpu.make_async_copy(a_hbm.at[:, cols], a_ref.at[j], sems.at[1, j]),
                pltpu.make_async_copy(b_hbm.at[:, cols], b_ref.at[j], sems.at[2, j]),
            )
        )
    for pair in copies:
        for copy in pair:
            copy.start()
    for j, (kind, dims) in enumerate(((0, NT), (1, NT), (1, NN))):
        for copy in copies[j]:
            copy.wait()
        for i in range(2):
            cols = slice(i * HD, (i + 1) * HD)
            h = 2 * core + i
            far = b_ref[j, :, cols].astype(BF16)
            term = dot(a_ref[j, :, cols], sa_ref[kind, h].astype(BF16), dims)
            term += dot(far, sb_ref[kind, h].astype(BF16), dims)
            s_ref[j, :, :, :, :, cols] = (w_ref[j, :, cols] + term).reshape(8, 4, 4, 8, HD)
        lanes = slice(j * HD, (j + 1) * HD)
        kept, sent = pick(at_ref, 0)
        for i in range(2):
            kx_ref[:, :, i, :, lanes] = s_ref[j, :, :, kept[i], :, 0:128]
            sx_ref[:, :, i, :, lanes] = s_ref[j, :, :, sent[i], :, 0:128]
        kept, sent = pick(at_ref, 1)
        for i in range(2):
            ky_ref[:, i, :, :, lanes] = s_ref[j, :, kept[i], :, :, 128:256]
            sy_ref[:, i, :, :, lanes] = s_ref[j, :, sent[i], :, :, 128:256]


def finish(at, w, a, b, sa, sb):
    vmem = pl.BlockSpec(memory_space=pltpu.VMEM)
    hbm = pl.BlockSpec(memory_space=pltpu.HBM)
    return pl.pallas_call(
        finish_body,
        in_specs=[pl.BlockSpec(memory_space=pltpu.SMEM), hbm, hbm, hbm, vmem, vmem],
        out_specs=[vmem] * 4,
        out_shape=[jax.ShapeDtypeStruct((8, 4, 2, 8, 384), F32)] * 2
        + [jax.ShapeDtypeStruct((8, 2, 4, 8, 384), F32)] * 2,
        scratch_shapes=[
            pltpu.VMEM((3, DM, 256), F32),
            pltpu.VMEM((3, DM, 256), BF16),
            pltpu.VMEM((3, DM, 256), F32),
            pltpu.VMEM((3, 8, 4, 4, 8, 256), F32),
            pltpu.SemaphoreType.DMA((3, 3)),
        ],
        compiler_params=params(49),
        cost_estimate=cost(1e9, 12e6),
        name="finish",
    )(at, w, a, b, sa, sb)


def inputs_body(loc_ref, qkv_ref, sg_ref, s_ref, w_ref, o_ref, d_ref):
    for h in range(H):
        before = s_ref[0, h].astype(BF16)
        after = s_ref[1, h].astype(BF16)
        parts = (
            dot(sg_ref[:, pl.ds(h * HD, HD)], before, NT),
            dot(qkv_ref[:, head(2, h)], after, NT),
            dot(qkv_ref[:, head(1, h)], after, NN),
        )
        for p, d in enumerate(parts):
            d_ref[:, head(p, h)] = (loc_ref[:, head(p, h)].astype(F32) + d).astype(BF16)
    o_ref[...] = dot(d_ref[...], w_ref[...], NT).astype(BF16)


def inputs_grad(loc, qkv, sg, states, weights):
    block = lambda cols: pl.BlockSpec((CH, cols), lambda n: (n, 0))
    return pl.pallas_call(
        inputs_body,
        grid=(NB,),
        in_specs=[
            block(3 * D),
            block(3 * D),
            block(D),
            pl.BlockSpec((2, H, HD, HD), lambda n: (0, 0, 0, 0)),
            pl.BlockSpec((DM, 3 * D), lambda n: (0, 0)),
        ],
        out_specs=block(DM),
        out_shape=jax.ShapeDtypeStruct((TOK, DM), BF16),
        scratch_shapes=[pltpu.VMEM((CH, 3 * D), BF16)],
        compiler_params=params(48),
        cost_estimate=cost(5e9, 14e6),
        name="inputs_grad",
    )(loc, qkv, sg, states, weights)


def whole_call(body, name, shapes, *args, scratch=()):
    vmem = pl.BlockSpec(memory_space=pltpu.VMEM)
    smem = pl.BlockSpec(memory_space=pltpu.SMEM)
    return pl.pallas_call(
        body,
        in_specs=[smem if a.dtype == jnp.int32 else vmem for a in args],
        out_specs=[vmem] * len(shapes),
        out_shape=[jax.ShapeDtypeStruct(s, F32) for s in shapes],
        scratch_shapes=list(scratch),
        compiler_params=params(16),
        name=name,
    )(*args)


def add1_body(kx, rx, ky, ry, kx2, sx2, ky2, sy2):
    kx2[...] = kx[:, :, 0] + rx[:, :, 0]
    sx2[...] = kx[:, :, 1] + rx[:, :, 1]
    ky2[...] = ky[:, 0] + ry[:, 0]
    sy2[...] = ky[:, 1] + ry[:, 1]


def add2_body(at, kx, rx, ky, ry, kp, sp, kq, sq):
    for axis, k, r, ko, so in ((1, kx, rx, kp, sp), (0, ky, ry, kq, sq)):
        kept, sent = pick(at, axis)
        for i in range(2):
            ko[:, i] = k[:, kept[i]] + r[:, kept[i]]
            so[:, i] = k[:, sent[i]] + r[:, sent[i]]


def add3_body(kp, rp, kq, rq, kp2, sp2, kq2, sq2):
    for k, r, ko, so in ((kp, rp, kp2, sp2), (kq, rq, kq2, sq2)):
        ko[...] = k[:, 0] + r[:, 0]
        so[...] = k[:, 1] + r[:, 1]


def add4_body(at, kp, rp, kq, rq, kz, sz):
    for o, first in ((kz, 9), (sz, 13)):
        for i in range(4):
            j = at[first + i]
            o[i, :, 0:384] = kp[j] + rp[j]
            o[i, :, 384:768] = kq[j] + rq[j]


def halve_body(k, r, ko, so):
    half = ko.shape[0]
    ko[...] = k[0:half] + r[0:half]
    so[...] = k[half:] + r[half:]


def add_body(k, r, o):
    o[...] = k[0] + r[0]


def rows_body(at, a0, a1, a2, a3, o):
    x = at[1]
    for d, a in enumerate((a0, a1, a2, a3)):
        o[(x + 4 - d) % 4] = a[...]


def place_body(at, mine, other, o):
    def put(core, a):
        for p in range(6):
            first = (p % 3) * 512 + core * 256 + (p // 3) * 128
            o[:, first : first + 128] = a[:, p * 128 : (p + 1) * 128]

    for core in range(2):

        @pl.when(at[0] == core)
        def _(core=core):
            put(core, mine)
            put(1 - core, other)


def exchange(value, axis, step):
    pairs = []
    for i in range(4):
        for c in range(2):
            j = i ^ ((1, 3), (3, 1))[c][step]
            pairs.append((2 * i + c, 2 * j + c))
    return lax.ppermute(value, (axis, "core"), pairs)


def along_z(z, core, step):
    up = (z ^ 1) if (core + step) % 2 == 0 else (((z + 1) ^ 1) + 7)
    return up % 8


def exchange_z(value, step):
    pairs = []
    for z in range(8):
        for c in range(2):
            partner = (z + 4) % 8 if step == 2 else along_z(z, c, step)
            pairs.append((2 * z + c, 2 * partner + c))
    return lax.ppermute(value, ("z", "core"), pairs)


def shards(inputs, weights, out_grad):
    x = inputs[0]
    z_at, y_at, x_at, core = (lax.axis_index(a) for a in ("z", "y", "x", "core"))
    tm_at = z_at * 4 + y_at
    first = jnp.where(core == 0, 1, 3)
    second = 4 - first
    one, two = (z_at ^ 1) % 8, (((z_at + 1) ^ 1) + 7) % 8
    z_first, z_second = jnp.where(core == 0, one, two), jnp.where(core == 0, two, one)
    z_both = jnp.where(core == 0, (((z_first + 1) ^ 1) + 7) % 8, z_first ^ 1)
    at = jnp.stack(
        [core]
        + [v for i in (x_at, y_at) for v in (i, i ^ first ^ second, i ^ first, i ^ second)]
        + [v % 8 for i in (z_at, z_second, z_first, z_both) for v in (i, i + 4)]
    ).astype(jnp.int32)
    offset = (tm_at * TOK).astype(jnp.int32)[None]
    back = (tm_at >= 16).astype(jnp.int32)[None]

    qkv, sg, kv, qg, total = project(offset, x, weights, out_grad[0])
    slices = lax.all_to_all(total.reshape(32, 32, HD), ("z", "y"), 0, 0, tiled=True)
    loc = local(qkv, sg, kv, qg)
    local_out = give(at, x, [(loc, 0), (loc, 2), (loc, 4)], "local_give")
    slices, local_out = lax.optimization_barrier((slices, local_out))
    local_in = lax.ppermute(local_out, "core", SWAP)

    scanned = scan_states(back, slices)
    scanned, sg, qkv, loc = lax.optimization_barrier((scanned, sg, qkv, loc))
    states = lax.all_to_all(scanned, ("z", "y"), 0, 0, tiled=True)
    factors_out = give(at, x, [(sg, 0), (qkv, 4), (qkv, 2)], "factors_give")
    factors_in = lax.ppermute(factors_out, "core", SWAP)
    both, mine = keep(at, x, local_in, [(loc, 0), (loc, 2), (loc, 4), (sg, 0), (qkv, 4), (qkv, 2)])
    states, mine, both = lax.optimization_barrier((states, mine, both))

    states = states.reshape(2, H, HD, HD)
    states_in = lax.ppermute(states, "core", SWAP)
    kx, sx, ky, sy = finish(at, both, mine, factors_in, states, states_in)
    rx = exchange(sx, "x", 0)
    ry = exchange(sy, "y", 0)
    record_grad = inputs_grad(loc, qkv, sg, states, weights)
    rx, ry, record_grad = lax.optimization_barrier((rx, ry, record_grad))
    kx, sx, ky, sy = whole_call(add1_body, "add1", [(8, 4, 8, 384)] * 4, kx, rx, ky, ry)
    rx = exchange(sx, "x", 1)
    ry = exchange(sy, "y", 1)
    kp, sp, kq, sq = whole_call(add2_body, "add2", [(8, 2, 8, 384)] * 4, at, kx, rx, ky, ry)
    rp = exchange(sp, "y", 0)
    rq = exchange(sq, "x", 0)
    kp, sp, kq, sq = whole_call(add3_body, "add3", [(8, 8, 384)] * 4, kp, rp, kq, rq)
    rp = exchange(sp, "y", 1)
    rq = exchange(sq, "x", 1)
    kz, sz = whole_call(add4_body, "add4", [(4, 8, 768)] * 2, at, kp, rp, kq, rq)
    kz, sz = whole_call(halve_body, "add5", [(2, 8, 768)] * 2, kz, exchange_z(sz, 0))
    kz, sz = whole_call(halve_body, "add6", [(1, 8, 768)] * 2, kz, exchange_z(sz, 1))
    (own,) = whole_call(add_body, "add7", [(8, 768)], kz, exchange_z(sz, 2))
    around = [own] + [
        lax.ppermute(own, "x", [(i, (i + d) % 4) for i in range(4)]) for d in range(1, 4)
    ]
    (rows,) = whole_call(rows_body, "rows", [(4, 8, 768)], at, *around)
    rows = rows.reshape(32, 768)
    other = lax.ppermute(rows, "core", SWAP)
    (proj_grad,) = whole_call(place_body, "place", [(32, 3 * D)], at, rows, other)
    return record_grad[None], proj_grad


def solution(mesh):
    fine = Mesh(mesh.devices.reshape(8, 4, 4, 2), ("z", "y", "x", "core"))
    tm, dp = ("z", "y"), ("x", "core")
    placed = (P(dp, tm, None), P(), P(dp, tm, None))
    return jax.shard_map(
        shards,
        mesh=fine,
        in_specs=placed,
        out_specs=(P(dp, tm, None), P(tm, None)),
        check_vma=False,
    )
```

```python
import functools

import jax
import jax.numpy as jnp
from jax import lax
from jax.experimental import pallas as pl
from jax.experimental.pallas import tpu as pltpu
from jax.sharding import Mesh, PartitionSpec as P

H = 4
HD = 128
CH = 256
NB = 4
D = H * HD
DM = 1024
TOK = NB * CH
F32 = jnp.float32
BF16 = jnp.bfloat16

NN = (((1,), (0,)), ((), ()))
NT = (((1,), (1,)), ((), ()))
TN = (((0,), (0,)), ((), ()))


def dot(a, b, dims):
    return lax.dot_general(a, b, dims, preferred_element_type=F32)


MIB = 1024 * 1024
SWAP = [(0, 1), (1, 0)]


def params(mib=40):
    return pltpu.CompilerParams(vmem_limit_bytes=mib * MIB)


def cost(flops, moved):
    return pl.CostEstimate(flops=int(flops), bytes_accessed=int(moved), transcendentals=0)


def head(part, h):
    return pl.ds(part * D + h * HD, HD)


def project_body(pos_ref, x_ref, w_ref, g_ref, qkv_ref, sg_ref, kv_ref, qg_ref, total_ref):
    n = pl.program_id(0)
    qkv_ref[...] = dot(x_ref[...], w_ref[...], NN).astype(BF16)
    pos = (pos_ref[0] + n * CH + lax.broadcasted_iota(jnp.int32, (CH, 1), 0)).astype(F32)
    factor = 1.0 / jnp.sqrt(jnp.float32(HD) * (pos + 1.0))
    sg_ref[...] = (g_ref[...].astype(F32) * factor).astype(BF16)

    @pl.when(n == 0)
    def _():
        total_ref[...] = jnp.zeros_like(total_ref)

    for h in range(H):
        kv = dot(qkv_ref[:, head(1, h)], qkv_ref[:, head(2, h)], TN)
        qg = dot(qkv_ref[:, head(0, h)], sg_ref[:, pl.ds(h * HD, HD)], TN)
        kv_ref[0, h] = kv
        qg_ref[0, h] = qg
        total_ref[0, h] += kv
        total_ref[1, h] += qg


def project(offset, x, w, g):
    block = lambda cols: pl.BlockSpec((CH, cols), lambda n, s: (n, 0))
    sums = pl.BlockSpec((1, H, HD, HD), lambda n, s: (n, 0, 0, 0))
    return pl.pallas_call(
        project_body,
        grid_spec=pltpu.PrefetchScalarGridSpec(
            num_scalar_prefetch=1,
            grid=(NB,),
            in_specs=[block(DM), pl.BlockSpec((DM, 3 * D), lambda n, s: (0, 0)), block(D)],
            out_specs=[
                block(3 * D),
                block(D),
                sums,
                sums,
                pl.BlockSpec((2, H, HD, HD), lambda n, s: (0, 0, 0, 0)),
            ],
        ),
        out_shape=[
            jax.ShapeDtypeStruct((TOK, 3 * D), BF16),
            jax.ShapeDtypeStruct((TOK, D), BF16),
            jax.ShapeDtypeStruct((NB, H, HD, HD), F32),
            jax.ShapeDtypeStruct((NB, H, HD, HD), F32),
            jax.ShapeDtypeStruct((2, H, HD, HD), F32),
        ],
        compiler_params=params(60),
        name="project",
    )(offset, x, w, g)


def scan_body(count, back_ref, v_ref, o_ref):

    def step(t, so_far):
        i = jnp.where(back_ref[0] == 1, count - 1 - t, t)
        o_ref[i] = so_far
        return so_far + v_ref[i]

    lax.fori_loop(0, count, step, jnp.zeros(v_ref.shape[1:], F32))


def scan_states(back, v):
    return pl.pallas_call(
        functools.partial(scan_body, v.shape[0]),
        in_specs=[pl.BlockSpec(memory_space=pltpu.SMEM), pl.BlockSpec(memory_space=pltpu.VMEM)],
        out_specs=pl.BlockSpec(memory_space=pltpu.VMEM),
        out_shape=jax.ShapeDtypeStruct(v.shape, F32),
        compiler_params=params(4),
        name="scan_states",
    )(back, v)


def local_body(at_ref, qkv_ref, sg_ref, kv_ref, qg_ref, x_ref, loc_ref, give_ref, from_ref):
    n = pl.program_id(0)
    theirs = pl.multiple_of((1 - at_ref[0]) * 256, 256)

    @pl.when(n < NB)
    def _():
        keep = lax.broadcasted_iota(jnp.int32, (CH, CH), 0) >= lax.broadcasted_iota(jnp.int32, (CH, CH), 1)
        for h in range(H):
            q, k, v = (qkv_ref[:, head(p, h)] for p in range(3))
            g = sg_ref[:, pl.ds(h * HD, HD)]
            before = jnp.zeros((HD, HD), F32)
            after = jnp.zeros((HD, HD), F32)
            for m in range(NB):
                before = before + jnp.where(m < n, kv_ref[m, h], 0.0)
                after = after + jnp.where(m > n, qg_ref[m, h], 0.0)
            before = before.astype(BF16)
            after = after.astype(BF16)
            mvg = jnp.where(keep, dot(g, v, NT), 0.0).astype(BF16)
            mqk = jnp.where(keep, dot(q, k, NT), 0.0).astype(BF16)
            dq = dot(mvg, k, NN) + dot(g, before, NT)
            dk = dot(mvg, q, TN) + dot(v, after, NT)
            dv = dot(mqk, g, TN) + dot(k, after, NN)
            for p, d in enumerate((dq, dk, dv)):
                loc_ref[:, head(p, h)] = d.astype(BF16)
        rows = pl.ds(pl.multiple_of(n * CH, CH), CH)
        for p in range(3):
            from_ref[rows, p * 256 : (p + 1) * 256] = loc_ref[:, pl.ds(p * D + theirs, 256)]
        from_ref[rows, 768:1024] = sg_ref[:, pl.ds(theirs, 256)]
        from_ref[rows, 1024:1280] = qkv_ref[:, pl.ds(2 * D + theirs, 256)]
        from_ref[rows, 1280:1536] = qkv_ref[:, pl.ds(D + theirs, 256)]

    @pl.when(n >= NB)
    def _():
        give_ref[...] = dot(x_ref[...], from_ref[...], TN)


def local(at, qkv, sg, kv, qg, x):
    first = lambda n: jnp.minimum(n, NB - 1)
    last = lambda n: jnp.maximum(n - NB, 0)
    block = lambda cols: pl.BlockSpec((CH, cols), lambda n, s: (first(n), 0))
    sums = pl.BlockSpec((NB, H, HD, HD), lambda n, s: (0, 0, 0, 0))
    return pl.pallas_call(
        local_body,
        grid_spec=pltpu.PrefetchScalarGridSpec(
            num_scalar_prefetch=1,
            grid=(2 * NB,),
            in_specs=[
                block(3 * D),
                block(D),
                sums,
                sums,
                pl.BlockSpec((TOK, DM // 4), lambda n, s: (0, last(n))),
            ],
            out_specs=[block(3 * D), pl.BlockSpec((DM // 4, 3 * D), lambda n, s: (last(n), 0))],
            scratch_shapes=[pltpu.VMEM((TOK, 3 * D), BF16)],
        ),
        out_shape=[
            jax.ShapeDtypeStruct((TOK, 3 * D), BF16),
            jax.ShapeDtypeStruct((DM, 3 * D), F32),
        ],
        compiler_params=params(60),
        cost_estimate=cost(8e9, 24e6),
        name="local",
    )(at, qkv, sg, kv, qg, x)


def keep_body(at_ref, x_ref, r_ref, *refs):
    w_ref, f_ref = refs[6:]
    for j in range(3):
        cols = slice(j * 256, (j + 1) * 256)
        w_ref[:, cols] = dot(x_ref[...], refs[j][...], TN) + r_ref[:, cols]
        f_ref[:, cols] = dot(x_ref[...], refs[3 + j][...], TN).astype(BF16)


def keep(at, x, arrived, sources):
    cols = [pl.BlockSpec((TOK, 256), lambda i, s, f=f: (0, f + s[0])) for _, f in sources]
    rows = pl.BlockSpec((DM // 4, 768), lambda i, s: (i, 0))
    return pl.pallas_call(
        keep_body,
        grid_spec=pltpu.PrefetchScalarGridSpec(
            num_scalar_prefetch=1,
            grid=(4,),
            in_specs=[pl.BlockSpec((TOK, DM // 4), lambda i, s: (0, i)), rows] + cols,
            out_specs=[rows, rows],
        ),
        out_shape=[jax.ShapeDtypeStruct((DM, 768), F32), jax.ShapeDtypeStruct((DM, 768), BF16)],
        compiler_params=params(60),
        cost_estimate=cost(5e9, 16e6),
        name="keep",
    )(at, x, arrived, *(a for a, _ in sources))


def pick(at_ref, axis):
    mine, far, first, second = (at_ref[1 + 4 * axis + i] for i in range(4))
    return (mine, second), (first, far)


def finish_body(at_ref, w_hbm, a_hbm, b_hbm, sa_ref, sb_ref, kx_ref, sx_ref, ky_ref, sy_ref, w_ref, a_ref, b_ref, s_ref, sems):
    core = at_ref[0]
    copies = []
    for j in range(3):
        cols = pl.ds(j * 256, 256)
        copies.append(
            (
                pltpu.make_async_copy(w_hbm.at[:, cols], w_ref.at[j], sems.at[0, j]),
                pltpu.make_async_copy(a_hbm.at[:, cols], a_ref.at[j], sems.at[1, j]),
                pltpu.make_async_copy(b_hbm.at[:, pl.ds(768 + j * 256, 256)], b_ref.at[j], sems.at[2, j]),
            )
        )
    for pair in copies:
        for copy in pair:
            copy.start()
    for j, (kind, dims) in enumerate(((0, NT), (1, NT), (1, NN))):
        for copy in copies[j]:
            copy.wait()
        for i in range(2):
            cols = slice(i * HD, (i + 1) * HD)
            h = 2 * core + i
            far = b_ref[j, :, cols].astype(BF16)
            term = dot(a_ref[j, :, cols], sa_ref[kind, h].astype(BF16), dims)
            term += dot(far, sb_ref[kind, h].astype(BF16), dims)
            s_ref[j, :, :, :, :, cols] = (w_ref[j, :, cols] + term).reshape(8, 4, 4, 8, HD)
        lanes = slice(j * HD, (j + 1) * HD)
        kept, sent = pick(at_ref, 0)
        for i in range(2):
            kx_ref[:, :, i, :, lanes] = s_ref[j, :, :, kept[i], :, 0:128]
            sx_ref[:, :, i, :, lanes] = s_ref[j, :, :, sent[i], :, 0:128]
        kept, sent = pick(at_ref, 1)
        for i in range(2):
            ky_ref[:, i, :, :, lanes] = s_ref[j, :, kept[i], :, :, 128:256]
            sy_ref[:, i, :, :, lanes] = s_ref[j, :, sent[i], :, :, 128:256]


def finish(at, w, a, b, sa, sb):
    vmem = pl.BlockSpec(memory_space=pltpu.VMEM)
    hbm = pl.BlockSpec(memory_space=pltpu.HBM)
    return pl.pallas_call(
        finish_body,
        in_specs=[pl.BlockSpec(memory_space=pltpu.SMEM), hbm, hbm, hbm, vmem, vmem],
        out_specs=[vmem] * 4,
        out_shape=[jax.ShapeDtypeStruct((8, 4, 2, 8, 384), F32)] * 2
        + [jax.ShapeDtypeStruct((8, 2, 4, 8, 384), F32)] * 2,
        scratch_shapes=[
            pltpu.VMEM((3, DM, 256), F32),
            pltpu.VMEM((3, DM, 256), BF16),
            pltpu.VMEM((3, DM, 256), F32),
            pltpu.VMEM((3, 8, 4, 4, 8, 256), F32),
            pltpu.SemaphoreType.DMA((3, 3)),
        ],
        compiler_params=params(49),
        cost_estimate=cost(1e9, 12e6),
        name="finish",
    )(at, w, a, b, sa, sb)


def inputs_body(loc_ref, qkv_ref, sg_ref, s_ref, w_ref, o_ref, d_ref):
    for h in range(H):
        before = s_ref[0, h].astype(BF16)
        after = s_ref[1, h].astype(BF16)
        parts = (
            dot(sg_ref[:, pl.ds(h * HD, HD)], before, NT),
            dot(qkv_ref[:, head(2, h)], after, NT),
            dot(qkv_ref[:, head(1, h)], after, NN),
        )
        for p, d in enumerate(parts):
            d_ref[:, head(p, h)] = (loc_ref[:, head(p, h)].astype(F32) + d).astype(BF16)
    o_ref[...] = dot(d_ref[...], w_ref[...], NT).astype(BF16)


def inputs_grad(loc, qkv, sg, states, weights):
    block = lambda cols: pl.BlockSpec((CH, cols), lambda n: (n, 0))
    return pl.pallas_call(
        inputs_body,
        grid=(NB,),
        in_specs=[
            block(3 * D),
            block(3 * D),
            block(D),
            pl.BlockSpec((2, H, HD, HD), lambda n: (0, 0, 0, 0)),
            pl.BlockSpec((DM, 3 * D), lambda n: (0, 0)),
        ],
        out_specs=block(DM),
        out_shape=jax.ShapeDtypeStruct((TOK, DM), BF16),
        scratch_shapes=[pltpu.VMEM((CH, 3 * D), BF16)],
        compiler_params=params(48),
        cost_estimate=cost(5e9, 14e6),
        name="inputs_grad",
    )(loc, qkv, sg, states, weights)


def whole_call(body, name, shapes, *args, scratch=()):
    vmem = pl.BlockSpec(memory_space=pltpu.VMEM)
    smem = pl.BlockSpec(memory_space=pltpu.SMEM)
    return pl.pallas_call(
        body,
        in_specs=[smem if a.dtype == jnp.int32 else vmem for a in args],
        out_specs=[vmem] * len(shapes),
        out_shape=[jax.ShapeDtypeStruct(s, F32) for s in shapes],
        scratch_shapes=list(scratch),
        compiler_params=params(16),
        name=name,
    )(*args)


def add1_body(k, r, ko, so):
    at = (slice(None), slice(None)) if k.shape[1] == 4 else (slice(None),)
    ko[...] = k[at + (0,)] + r[at + (0,)]
    so[...] = k[at + (1,)] + r[at + (1,)]


def add2_body(axis, at, k, r, ko, so):
    kept, sent = pick(at, axis)
    for i in range(2):
        ko[:, i] = k[:, kept[i]] + r[:, kept[i]]
        so[:, i] = k[:, sent[i]] + r[:, sent[i]]


def add3_body(k, r, ko, so):
    ko[...] = k[:, 0] + r[:, 0]
    so[...] = k[:, 1] + r[:, 1]


def add4_body(kp, rp, kq, rq, o):
    o[:, :, 0:384] = kp[...] + rp[...]
    o[:, :, 384:768] = kq[...] + rq[...]


def sum_body(v, o):
    total = v[0]
    for i in range(1, v.shape[0]):
        total = total + v[i]
    for i in range(o.shape[0]):
        o[i] = total


def place_body(v, o):
    for i in range(8):
        for p in range(6):
            at = (p % 3) * 512 + (i % 2) * 256 + (p // 3) * 128
            o[i // 2 * 8 : i // 2 * 8 + 8, at : at + 128] = v[i, :, p * 128 : (p + 1) * 128]


def exchange(value, axis, step):
    pairs = []
    for i in range(4):
        for c in range(2):
            j = i ^ ((1, 3), (3, 1))[c][step]
            pairs.append((2 * i + c, 2 * j + c))
    return lax.ppermute(value, (axis, "core"), pairs)


def shards(inputs, weights, out_grad):
    x = inputs[0]
    z_at, y_at, x_at, core = (lax.axis_index(a) for a in ("z", "y", "x", "core"))
    tm_at = z_at * 4 + y_at
    first = jnp.where(core == 0, 1, 3)
    second = 4 - first
    at = jnp.stack(
        [core]
        + [v for i in (x_at, y_at) for v in (i, i ^ first ^ second, i ^ first, i ^ second)]
    ).astype(jnp.int32)
    offset = (tm_at * TOK).astype(jnp.int32)[None]
    back = (tm_at >= 16).astype(jnp.int32)[None]

    qkv, sg, kv, qg, total = project(offset, x, weights, out_grad[0])
    slices = lax.all_to_all(total.reshape(32, 32, HD), ("z", "y"), 0, 0, tiled=True)
    loc, given = local(at, qkv, sg, kv, qg, x)
    slices, given = lax.optimization_barrier((slices, given))
    arrived = lax.ppermute(given, "core", SWAP)

    scanned = scan_states(back, slices)
    states = lax.all_to_all(scanned, ("z", "y"), 0, 0, tiled=True)
    both, mine = keep(at, x, arrived, [(loc, 0), (loc, 2), (loc, 4), (sg, 0), (qkv, 4), (qkv, 2)])
    states, mine, both = lax.optimization_barrier((states, mine, both))

    states = states.reshape(2, H, HD, HD)
    states_in = lax.ppermute(states, "core", SWAP)
    kx, sx, ky, sy = finish(at, both, mine, arrived, states, states_in)
    rx = exchange(sx, "x", 0)
    ry = exchange(sy, "y", 0)
    record_grad = inputs_grad(loc, qkv, sg, states, weights)
    rx, ry, record_grad = lax.optimization_barrier((rx, ry, record_grad))
    kp, sp = whole_call(add1_body, "add1x", [(8, 4, 8, 384)] * 2, kx, rx)
    rp = exchange(sp, "x", 1)
    kq, sq = whole_call(add1_body, "add1y", [(8, 4, 8, 384)] * 2, ky, ry)
    rq = exchange(sq, "y", 1)
    kp, sp = whole_call(functools.partial(add2_body, 1), "add2x", [(8, 2, 8, 384)] * 2, at, kp, rp)
    rp = exchange(sp, "y", 0)
    kq, sq = whole_call(functools.partial(add2_body, 0), "add2y", [(8, 2, 8, 384)] * 2, at, kq, rq)
    rq = exchange(sq, "x", 0)
    kp, sp = whole_call(add3_body, "add3x", [(8, 8, 384)] * 2, kp, rp)
    rp = exchange(sp, "y", 1)
    kq, sq = whole_call(add3_body, "add3y", [(8, 8, 384)] * 2, kq, rq)
    rq = exchange(sq, "x", 1)
    (part,) = whole_call(add4_body, "add4", [(8, 8, 768)], kp, rp, kq, rq)
    part = lax.all_to_all(part, "z", 0, 0, tiled=True)
    (own,) = whole_call(sum_body, "sum_z", [(8, 8, 768)], part)
    rows = lax.all_to_all(own, ("x", "core"), 0, 0, tiled=True)
    (proj_grad,) = whole_call(place_body, "place", [(32, 3 * D)], rows)
    return record_grad[None], proj_grad


def solution(mesh):
    fine = Mesh(mesh.devices.reshape(8, 4, 4, 2), ("z", "y", "x", "core"))
    tm, dp = ("z", "y"), ("x", "core")
    placed = (P(dp, tm, None), P(), P(dp, tm, None))
    return jax.shard_map(
        shards,
        mesh=fine,
        in_specs=placed,
        out_specs=(P(dp, tm, None), P(tm, None)),
        check_vma=False,
    )
```

```python
import functools

import jax
import jax.numpy as jnp
from jax import lax
from jax.experimental import pallas as pl
from jax.experimental.pallas import tpu as pltpu
from jax.sharding import Mesh, PartitionSpec as P

H = 4
HD = 128
CH = 256
NB = 4
D = H * HD
DM = 1024
TOK = NB * CH
F32 = jnp.float32
BF16 = jnp.bfloat16

NN = (((1,), (0,)), ((), ()))
NT = (((1,), (1,)), ((), ()))
TN = (((0,), (0,)), ((), ()))


def dot(a, b, dims):
    return lax.dot_general(a, b, dims, preferred_element_type=F32)


MIB = 1024 * 1024
SWAP = [(0, 1), (1, 0)]


def params(mib=40):
    return pltpu.CompilerParams(vmem_limit_bytes=mib * MIB)


def cost(flops, moved):
    return pl.CostEstimate(flops=int(flops), bytes_accessed=int(moved), transcendentals=0)


def head(part, h):
    return pl.ds(part * D + h * HD, HD)


def project_body(at_ref, x_ref, w_ref, g_ref, qkv_ref, sg_ref, kv_ref, qg_ref, total_ref):
    n = pl.program_id(0)
    qkv_ref[...] = dot(x_ref[...], w_ref[...], NN).astype(BF16)
    pos = (at_ref[9] + n * CH + lax.broadcasted_iota(jnp.int32, (CH, 1), 0)).astype(F32)
    factor = 1.0 / jnp.sqrt(jnp.float32(HD) * (pos + 1.0))
    sg_ref[...] = (g_ref[...].astype(F32) * factor).astype(BF16)

    @pl.when(n == 0)
    def _():
        total_ref[...] = jnp.zeros_like(total_ref)

    for h in range(H):
        kv = dot(qkv_ref[:, head(1, h)], qkv_ref[:, head(2, h)], TN)
        qg = dot(qkv_ref[:, head(0, h)], sg_ref[:, pl.ds(h * HD, HD)], TN)
        kv_ref[0, h] = kv
        qg_ref[0, h] = qg
        total_ref[0, h] += kv
        total_ref[1, h] += qg


def project(at, x, w, g):
    block = lambda cols: pl.BlockSpec((CH, cols), lambda n, s: (n, 0))
    sums = pl.BlockSpec((1, H, HD, HD), lambda n, s: (n, 0, 0, 0))
    return pl.pallas_call(
        project_body,
        grid_spec=pltpu.PrefetchScalarGridSpec(
            num_scalar_prefetch=1,
            grid=(NB,),
            in_specs=[block(DM), pl.BlockSpec((DM, 3 * D), lambda n, s: (0, 0)), block(D)],
            out_specs=[
                block(3 * D),
                block(D),
                sums,
                sums,
                pl.BlockSpec((2, H, HD, HD), lambda n, s: (0, 0, 0, 0)),
            ],
        ),
        out_shape=[
            jax.ShapeDtypeStruct((TOK, 3 * D), BF16),
            jax.ShapeDtypeStruct((TOK, D), BF16),
            jax.ShapeDtypeStruct((NB, H, HD, HD), F32),
            jax.ShapeDtypeStruct((NB, H, HD, HD), F32),
            jax.ShapeDtypeStruct((2, H, HD, HD), F32),
        ],
        compiler_params=params(60),
        name="project",
    )(at, x, w, g)


def scan_body(count, at_ref, v_ref, o_ref):

    def step(t, so_far):
        i = jnp.where(at_ref[10] == 1, count - 1 - t, t)
        o_ref[i] = so_far
        return so_far + v_ref[i]

    lax.fori_loop(0, count, step, jnp.zeros(v_ref.shape[1:], F32))


def scan_states(at, v):
    return pl.pallas_call(
        functools.partial(scan_body, v.shape[0]),
        in_specs=[pl.BlockSpec(memory_space=pltpu.SMEM), pl.BlockSpec(memory_space=pltpu.VMEM)],
        out_specs=pl.BlockSpec(memory_space=pltpu.VMEM),
        out_shape=jax.ShapeDtypeStruct(v.shape, F32),
        compiler_params=params(4),
        name="scan_states",
    )(at, v)


def local_body(at_ref, qkv_ref, sg_ref, kv_ref, qg_ref, x_hbm, loc_ref, give_ref, from_ref, x_ref, sem):
    n = pl.program_id(0)
    copy = pltpu.make_async_copy(x_hbm, x_ref, sem)
    theirs = pl.multiple_of((1 - at_ref[0]) * 256, 256)

    @pl.when(n == 0)
    def _():
        copy.start()

    @pl.when(n < NB)
    def _():
        keep = lax.broadcasted_iota(jnp.int32, (CH, CH), 0) >= lax.broadcasted_iota(jnp.int32, (CH, CH), 1)
        for h in range(H):
            q, k, v = (qkv_ref[:, head(p, h)] for p in range(3))
            g = sg_ref[:, pl.ds(h * HD, HD)]
            before = jnp.zeros((HD, HD), F32)
            after = jnp.zeros((HD, HD), F32)
            for m in range(NB):
                before = before + jnp.where(m < n, kv_ref[m, h], 0.0)
                after = after + jnp.where(m > n, qg_ref[m, h], 0.0)
            before = before.astype(BF16)
            after = after.astype(BF16)
            mvg = jnp.where(keep, dot(g, v, NT), 0.0).astype(BF16)
            mqk = jnp.where(keep, dot(q, k, NT), 0.0).astype(BF16)
            dq = dot(mvg, k, NN) + dot(g, before, NT)
            dk = dot(mvg, q, TN) + dot(v, after, NT)
            dv = dot(mqk, g, TN) + dot(k, after, NN)
            for p, d in enumerate((dq, dk, dv)):
                loc_ref[:, head(p, h)] = d.astype(BF16)
        rows = pl.ds(pl.multiple_of(n * CH, CH), CH)
        for p in range(3):
            from_ref[rows, p * 256 : (p + 1) * 256] = loc_ref[:, pl.ds(p * D + theirs, 256)]

    @pl.when(n == NB)
    def _():
        copy.wait()

    @pl.when(n >= NB)
    def _():
        half = pl.ds(pl.multiple_of((n - NB) * (DM // 2), DM // 2), DM // 2)
        give_ref[...] = dot(x_ref[:, half], from_ref[...], TN)


def local(at, qkv, sg, kv, qg, x):
    first = lambda n: jnp.minimum(n, NB - 1)
    last = lambda n: jnp.maximum(n - NB, 0)
    block = lambda cols: pl.BlockSpec((CH, cols), lambda n, s: (first(n), 0))
    sums = pl.BlockSpec((NB, H, HD, HD), lambda n, s: (0, 0, 0, 0))
    return pl.pallas_call(
        local_body,
        grid_spec=pltpu.PrefetchScalarGridSpec(
            num_scalar_prefetch=1,
            grid=(NB + 2,),
            in_specs=[
                block(3 * D),
                block(D),
                sums,
                sums,
                pl.BlockSpec(memory_space=pltpu.HBM),
            ],
            out_specs=[block(3 * D), pl.BlockSpec((DM // 2, 768), lambda n, s: (last(n), 0))],
            scratch_shapes=[
                pltpu.VMEM((TOK, 768), BF16),
                pltpu.VMEM((TOK, DM), BF16),
                pltpu.SemaphoreType.DMA,
            ],
        ),
        out_shape=[
            jax.ShapeDtypeStruct((TOK, 3 * D), BF16),
            jax.ShapeDtypeStruct((DM, 768), F32),
        ],
        compiler_params=params(60),
        cost_estimate=cost(8e9, 24e6),
        name="local",
    )(at, qkv, sg, kv, qg, x)


def factors_body(at_ref, x_ref, *refs):
    for j, ref in enumerate(refs[:3]):
        refs[3][:, j * 256 : (j + 1) * 256] = dot(x_ref[...], ref[...], TN)


def factors(at, x, sources):
    cols = [pl.BlockSpec((TOK, 256), lambda i, s, f=f: (0, f + 1 - s[0])) for _, f in sources]
    return pl.pallas_call(
        factors_body,
        grid_spec=pltpu.PrefetchScalarGridSpec(
            num_scalar_prefetch=1,
            grid=(2,),
            in_specs=[pl.BlockSpec((TOK, DM // 2), lambda i, s: (0, i))] + cols,
            out_specs=pl.BlockSpec((DM // 2, 768), lambda i, s: (i, 0)),
        ),
        out_shape=jax.ShapeDtypeStruct((DM, 768), F32),
        compiler_params=params(60),
        cost_estimate=cost(3e9, 12e6),
        name="factors",
    )(at, x, *(a for a, _ in sources))


def keep_body(at_ref, x_ref, r_ref, *refs):
    w_ref, f_ref = refs[6:]
    for j in range(3):
        cols = slice(j * 256, (j + 1) * 256)
        w_ref[:, cols] = dot(x_ref[...], refs[j][...], TN) + r_ref[:, cols]
        f_ref[:, cols] = dot(x_ref[...], refs[3 + j][...], TN).astype(BF16)


def keep(at, x, arrived, sources):
    cols = [pl.BlockSpec((TOK, 256), lambda i, s, f=f: (0, f + s[0])) for _, f in sources]
    rows = pl.BlockSpec((DM // 2, 768), lambda i, s: (i, 0))
    return pl.pallas_call(
        keep_body,
        grid_spec=pltpu.PrefetchScalarGridSpec(
            num_scalar_prefetch=1,
            grid=(2,),
            in_specs=[pl.BlockSpec((TOK, DM // 2), lambda i, s: (0, i)), rows] + cols,
            out_specs=[rows, rows],
        ),
        out_shape=[jax.ShapeDtypeStruct((DM, 768), F32), jax.ShapeDtypeStruct((DM, 768), BF16)],
        compiler_params=params(60),
        cost_estimate=cost(40e9, 16e6),
        name="keep",
    )(at, x, arrived, *(a for a, _ in sources))


def pick(at_ref, axis):
    mine, far, first, second = (at_ref[1 + 4 * axis + i] for i in range(4))
    return (mine, second), (first, far)


def finish_body(at_ref, w_hbm, a_hbm, b_hbm, sa_ref, sb_ref, kx_ref, sx_ref, ky_ref, sy_ref, w_ref, a_ref, b_ref, s_ref, sems):
    core = at_ref[0]
    copies = []
    for j in range(3):
        cols = pl.ds(j * 256, 256)
        copies.append(
            (
                pltpu.make_async_copy(w_hbm.at[:, cols], w_ref.at[j], sems.at[0, j]),
                pltpu.make_async_copy(a_hbm.at[:, cols], a_ref.at[j], sems.at[1, j]),
                pltpu.make_async_copy(b_hbm.at[:, cols], b_ref.at[j], sems.at[2, j]),
            )
        )
    for pair in copies:
        for copy in pair:
            copy.start()
    for j, (kind, dims) in enumerate(((0, NT), (1, NT), (1, NN))):
        for copy in copies[j]:
            copy.wait()
        for i in range(2):
            cols = slice(i * HD, (i + 1) * HD)
            h = 2 * core + i
            far = b_ref[j, :, cols].astype(BF16)
            term = dot(a_ref[j, :, cols], sa_ref[kind, h].astype(BF16), dims)
            term += dot(far, sb_ref[kind, h].astype(BF16), dims)
            s_ref[j, :, :, :, :, cols] = (w_ref[j, :, cols] + term).reshape(8, 4, 4, 8, HD)
        lanes = slice(j * HD, (j + 1) * HD)
        kept, sent = pick(at_ref, 0)
        for i in range(2):
            kx_ref[:, :, i, :, lanes] = s_ref[j, :, :, kept[i], :, 0:128]
            sx_ref[:, :, i, :, lanes] = s_ref[j, :, :, sent[i], :, 0:128]
        kept, sent = pick(at_ref, 1)
        for i in range(2):
            ky_ref[:, i, :, :, lanes] = s_ref[j, :, kept[i], :, :, 128:256]
            sy_ref[:, i, :, :, lanes] = s_ref[j, :, sent[i], :, :, 128:256]


def finish(at, w, a, b, sa, sb):
    vmem = pl.BlockSpec(memory_space=pltpu.VMEM)
    hbm = pl.BlockSpec(memory_space=pltpu.HBM)
    return pl.pallas_call(
        finish_body,
        in_specs=[pl.BlockSpec(memory_space=pltpu.SMEM), hbm, hbm, hbm, vmem, vmem],
        out_specs=[vmem] * 4,
        out_shape=[jax.ShapeDtypeStruct((8, 4, 2, 8, 384), F32)] * 2
        + [jax.ShapeDtypeStruct((8, 2, 4, 8, 384), F32)] * 2,
        scratch_shapes=[
            pltpu.VMEM((3, DM, 256), F32),
            pltpu.VMEM((3, DM, 256), BF16),
            pltpu.VMEM((3, DM, 256), F32),
            pltpu.VMEM((3, 8, 4, 4, 8, 256), F32),
            pltpu.SemaphoreType.DMA((3, 3)),
        ],
        compiler_params=params(49),
        cost_estimate=cost(1e9, 12e6),
        name="finish",
    )(at, w, a, b, sa, sb)


def inputs_body(loc_ref, qkv_ref, sg_ref, s_ref, w_ref, o_ref, d_ref):
    for h in range(H):
        before = s_ref[0, h].astype(BF16)
        after = s_ref[1, h].astype(BF16)
        parts = (
            dot(sg_ref[:, pl.ds(h * HD, HD)], before, NT),
            dot(qkv_ref[:, head(2, h)], after, NT),
            dot(qkv_ref[:, head(1, h)], after, NN),
        )
        for p, d in enumerate(parts):
            d_ref[:, head(p, h)] = (loc_ref[:, head(p, h)].astype(F32) + d).astype(BF16)
    o_ref[...] = dot(d_ref[...], w_ref[...], NT).astype(BF16)


def inputs_grad(loc, qkv, sg, states, weights):
    block = lambda cols: pl.BlockSpec((CH, cols), lambda n: (n, 0))
    return pl.pallas_call(
        inputs_body,
        grid=(NB,),
        in_specs=[
            block(3 * D),
            block(3 * D),
            block(D),
            pl.BlockSpec((2, H, HD, HD), lambda n: (0, 0, 0, 0)),
            pl.BlockSpec((DM, 3 * D), lambda n: (0, 0)),
        ],
        out_specs=block(DM),
        out_shape=jax.ShapeDtypeStruct((TOK, DM), BF16),
        scratch_shapes=[pltpu.VMEM((CH, 3 * D), BF16)],
        compiler_params=params(48),
        cost_estimate=cost(5e9, 14e6),
        name="inputs_grad",
    )(loc, qkv, sg, states, weights)


def whole_call(body, name, shapes, *args, scratch=()):
    vmem = pl.BlockSpec(memory_space=pltpu.VMEM)
    smem = pl.BlockSpec(memory_space=pltpu.SMEM)
    return pl.pallas_call(
        body,
        in_specs=[smem if a.dtype == jnp.int32 else vmem for a in args],
        out_specs=[vmem] * len(shapes),
        out_shape=[jax.ShapeDtypeStruct(s, F32) for s in shapes],
        scratch_shapes=list(scratch),
        compiler_params=params(16),
        name=name,
    )(*args)


def add1_body(k, r, ko, so):
    at = (slice(None), slice(None)) if k.shape[1] == 4 else (slice(None),)
    ko[...] = k[at + (0,)] + r[at + (0,)]
    so[...] = k[at + (1,)] + r[at + (1,)]


def add2_body(axis, at, k, r, ko, so):
    kept, sent = pick(at, axis)
    for i in range(2):
        ko[:, i] = k[:, kept[i]] + r[:, kept[i]]
        so[:, i] = k[:, sent[i]] + r[:, sent[i]]


def add3_body(k, r, ko, so):
    ko[...] = k[:, 0] + r[:, 0]
    so[...] = k[:, 1] + r[:, 1]


def add4_body(kp, rp, kq, rq, o):
    o[:, :, 0:384] = kp[...] + rp[...]
    o[:, :, 384:768] = kq[...] + rq[...]


def sum_body(v, o):
    total = v[0]
    for i in range(1, v.shape[0]):
        total = total + v[i]
    for i in range(o.shape[0]):
        o[i] = total


def place_body(v, o):
    for i in range(8):
        for p in range(6):
            at = (p % 3) * 512 + (i % 2) * 256 + (p // 3) * 128
            o[i // 2 * 8 : i // 2 * 8 + 8, at : at + 128] = v[i, :, p * 128 : (p + 1) * 128]


def exchange(value, axis, step):
    pairs = []
    for i in range(4):
        for c in range(2):
            j = i ^ ((1, 3), (3, 1))[c][step]
            pairs.append((2 * i + c, 2 * j + c))
    return lax.ppermute(value, (axis, "core"), pairs)


def shards(inputs, weights, out_grad):
    x = inputs[0]
    z_at, y_at, x_at, core = (lax.axis_index(a) for a in ("z", "y", "x", "core"))
    tm_at = z_at * 4 + y_at
    first = jnp.where(core == 0, 1, 3)
    second = 4 - first
    at = jnp.stack(
        [core]
        + [v for i in (x_at, y_at) for v in (i, i ^ first ^ second, i ^ first, i ^ second)]
        + [tm_at * TOK, (tm_at >= 16).astype(jnp.int32)]
    ).astype(jnp.int32)

    qkv, sg, kv, qg, total = project(at, x, weights, out_grad[0])
    slices = lax.all_to_all(total.reshape(32, 32, HD), ("z", "y"), 0, 0, tiled=True)
    loc, given = local(at, qkv, sg, kv, qg, x)
    slices, given = lax.optimization_barrier((slices, given))
    local_in = lax.ppermute(given, "core", SWAP)

    scanned = scan_states(at, slices)
    scanned, sg, qkv, loc = lax.optimization_barrier((scanned, sg, qkv, loc))
    states = lax.all_to_all(scanned, ("z", "y"), 0, 0, tiled=True)
    given = factors(at, x, [(sg, 0), (qkv, 4), (qkv, 2)])
    factors_in = lax.ppermute(given, "core", SWAP)
    both, mine = keep(at, x, local_in, [(loc, 0), (loc, 2), (loc, 4), (sg, 0), (qkv, 4), (qkv, 2)])
    states, mine, both = lax.optimization_barrier((states, mine, both))

    states = states.reshape(2, H, HD, HD)
    states_in = lax.ppermute(states, "core", SWAP)
    kx, sx, ky, sy = finish(at, both, mine, factors_in, states, states_in)
    rx = exchange(sx, "x", 0)
    ry = exchange(sy, "y", 0)
    record_grad = inputs_grad(loc, qkv, sg, states, weights)
    rx, ry, record_grad = lax.optimization_barrier((rx, ry, record_grad))
    kp, sp = whole_call(add1_body, "add1x", [(8, 4, 8, 384)] * 2, kx, rx)
    rp = exchange(sp, "x", 1)
    kq, sq = whole_call(add1_body, "add1y", [(8, 4, 8, 384)] * 2, ky, ry)
    rq = exchange(sq, "y", 1)
    kp, sp = whole_call(functools.partial(add2_body, 1), "add2x", [(8, 2, 8, 384)] * 2, at, kp, rp)
    rp = exchange(sp, "y", 0)
    kq, sq = whole_call(functools.partial(add2_body, 0), "add2y", [(8, 2, 8, 384)] * 2, at, kq, rq)
    rq = exchange(sq, "x", 0)
    kp, sp = whole_call(add3_body, "add3x", [(8, 8, 384)] * 2, kp, rp)
    rp = exchange(sp, "y", 1)
    kq, sq = whole_call(add3_body, "add3y", [(8, 8, 384)] * 2, kq, rq)
    rq = exchange(sq, "x", 1)
    (part,) = whole_call(add4_body, "add4", [(8, 8, 768)], kp, rp, kq, rq)
    part = lax.all_to_all(part, "z", 0, 0, tiled=True)
    (own,) = whole_call(sum_body, "sum_z", [(8, 8, 768)], part)
    rows = lax.all_to_all(own, ("x", "core"), 0, 0, tiled=True)
    (proj_grad,) = whole_call(place_body, "place", [(32, 3 * D)], rows)
    return record_grad[None], proj_grad


def solution(mesh):
    fine = Mesh(mesh.devices.reshape(8, 4, 4, 2), ("z", "y", "x", "core"))
    tm, dp = ("z", "y"), ("x", "core")
    placed = (P(dp, tm, None), P(), P(dp, tm, None))
    return jax.shard_map(
        shards,
        mesh=fine,
        in_specs=placed,
        out_specs=(P(dp, tm, None), P(tm, None)),
        check_vma=False,
    )
```

```python
import functools

import jax
import jax.numpy as jnp
from jax import lax
from jax.experimental import pallas as pl
from jax.experimental.pallas import tpu as pltpu
from jax.sharding import Mesh, PartitionSpec as P

H = 4
HD = 128
CH = 256
NB = 4
D = H * HD
DM = 1024
TOK = NB * CH
F32 = jnp.float32
BF16 = jnp.bfloat16

NN = (((1,), (0,)), ((), ()))
NT = (((1,), (1,)), ((), ()))
TN = (((0,), (0,)), ((), ()))


def dot(a, b, dims):
    return lax.dot_general(a, b, dims, preferred_element_type=F32)


MIB = 1024 * 1024
SWAP = [(0, 1), (1, 0)]


def params(mib=40):
    return pltpu.CompilerParams(vmem_limit_bytes=mib * MIB)


def cost(flops, moved):
    return pl.CostEstimate(flops=int(flops), bytes_accessed=int(moved), transcendentals=0)


def head(part, h):
    return pl.ds(part * D + h * HD, HD)


def project_body(x_ref, w_ref, g_ref, qkv_ref, sg_ref, kv_ref, qg_ref, total_ref):
    n = pl.program_id(0)
    first = (lax.axis_index("z") * 4 + lax.axis_index("y")) * TOK
    qkv_ref[...] = dot(x_ref[...], w_ref[...], NN).astype(BF16)
    pos = (first + n * CH + lax.broadcasted_iota(jnp.int32, (CH, 1), 0)).astype(F32)
    factor = 1.0 / jnp.sqrt(jnp.float32(HD) * (pos + 1.0))
    sg_ref[...] = (g_ref[...].astype(F32) * factor).astype(BF16)

    @pl.when(n == 0)
    def _():
        total_ref[...] = jnp.zeros_like(total_ref)

    for h in range(H):
        kv = dot(qkv_ref[:, head(1, h)], qkv_ref[:, head(2, h)], TN)
        qg = dot(qkv_ref[:, head(0, h)], sg_ref[:, pl.ds(h * HD, HD)], TN)
        kv_ref[0, h] = kv
        qg_ref[0, h] = qg
        total_ref[0, h] += kv
        total_ref[1, h] += qg


def project(x, w, g):
    block = lambda cols: pl.BlockSpec((CH, cols), lambda n: (n, 0))
    sums = pl.BlockSpec((1, H, HD, HD), lambda n: (n, 0, 0, 0))
    return pl.pallas_call(
        project_body,
            grid=(NB,),
            in_specs=[block(DM), pl.BlockSpec((DM, 3 * D), lambda n: (0, 0)), block(D)],
            out_specs=[
                block(3 * D),
                block(D),
                sums,
                sums,
                pl.BlockSpec((2, H, HD, HD), lambda n: (0, 0, 0, 0)),
            ],
        out_shape=[
            jax.ShapeDtypeStruct((TOK, 3 * D), BF16),
            jax.ShapeDtypeStruct((TOK, D), BF16),
            jax.ShapeDtypeStruct((NB, H, HD, HD), F32),
            jax.ShapeDtypeStruct((NB, H, HD, HD), F32),
            jax.ShapeDtypeStruct((2, H, HD, HD), F32),
        ],
        compiler_params=params(60),
        name="project",
    )(x, w, g)


def scan_body(count, v_ref, o_ref):
    back = lax.axis_index("z") >= 4


    def step(t, so_far):
        i = jnp.where(back, count - 1 - t, t)
        o_ref[i] = so_far
        return so_far + v_ref[i]

    lax.fori_loop(0, count, step, jnp.zeros(v_ref.shape[1:], F32))


def scan_states(v):
    return pl.pallas_call(
        functools.partial(scan_body, v.shape[0]),
        in_specs=[pl.BlockSpec(memory_space=pltpu.VMEM)],
        out_specs=pl.BlockSpec(memory_space=pltpu.VMEM),
        out_shape=jax.ShapeDtypeStruct(v.shape, F32),
        compiler_params=params(4),
        name="scan_states",
    )(v)


def local_body(at_ref, qkv_ref, sg_ref, kv_ref, qg_ref, x_hbm, loc_ref, give_ref, from_ref, x_ref, sem):
    n = pl.program_id(0)
    copy = pltpu.make_async_copy(x_hbm, x_ref, sem)
    theirs = pl.multiple_of((1 - at_ref[0]) * 256, 256)

    @pl.when(n == 0)
    def _():
        copy.start()

    @pl.when(n < NB)
    def _():
        keep = lax.broadcasted_iota(jnp.int32, (CH, CH), 0) >= lax.broadcasted_iota(jnp.int32, (CH, CH), 1)
        for h in range(H):
            q, k, v = (qkv_ref[:, head(p, h)] for p in range(3))
            g = sg_ref[:, pl.ds(h * HD, HD)]
            before = jnp.zeros((HD, HD), F32)
            after = jnp.zeros((HD, HD), F32)
            for m in range(NB):
                before = before + jnp.where(m < n, kv_ref[m, h], 0.0)
                after = after + jnp.where(m > n, qg_ref[m, h], 0.0)
            before = before.astype(BF16)
            after = after.astype(BF16)
            mvg = jnp.where(keep, dot(g, v, NT), 0.0).astype(BF16)
            mqk = jnp.where(keep, dot(q, k, NT), 0.0).astype(BF16)
            dq = dot(mvg, k, NN) + dot(g, before, NT)
            dk = dot(mvg, q, TN) + dot(v, after, NT)
            dv = dot(mqk, g, TN) + dot(k, after, NN)
            for p, d in enumerate((dq, dk, dv)):
                loc_ref[:, head(p, h)] = d.astype(BF16)
        rows = pl.ds(pl.multiple_of(n * CH, CH), CH)
        for p in range(3):
            from_ref[rows, p * 256 : (p + 1) * 256] = loc_ref[:, pl.ds(p * D + theirs, 256)]

    @pl.when(n == NB)
    def _():
        copy.wait()

    @pl.when(n >= NB)
    def _():
        half = pl.ds(pl.multiple_of((n - NB) * (DM // 2), DM // 2), DM // 2)
        give_ref[...] = dot(x_ref[:, half], from_ref[...], TN)


def local(at, qkv, sg, kv, qg, x):
    first = lambda n: jnp.minimum(n, NB - 1)
    last = lambda n: jnp.maximum(n - NB, 0)
    block = lambda cols: pl.BlockSpec((CH, cols), lambda n, s: (first(n), 0))
    sums = pl.BlockSpec((NB, H, HD, HD), lambda n, s: (0, 0, 0, 0))
    return pl.pallas_call(
        local_body,
        grid_spec=pltpu.PrefetchScalarGridSpec(
            num_scalar_prefetch=1,
            grid=(NB + 2,),
            in_specs=[
                block(3 * D),
                block(D),
                sums,
                sums,
                pl.BlockSpec(memory_space=pltpu.HBM),
            ],
            out_specs=[block(3 * D), pl.BlockSpec((DM // 2, 768), lambda n, s: (last(n), 0))],
            scratch_shapes=[
                pltpu.VMEM((TOK, 768), BF16),
                pltpu.VMEM((TOK, DM), BF16),
                pltpu.SemaphoreType.DMA,
            ],
        ),
        out_shape=[
            jax.ShapeDtypeStruct((TOK, 3 * D), BF16),
            jax.ShapeDtypeStruct((DM, 768), F32),
        ],
        compiler_params=params(60),
        cost_estimate=cost(8e9, 24e6),
        name="local",
    )(at, qkv, sg, kv, qg, x)


def factors_body(at_ref, x_ref, *refs):
    for j, ref in enumerate(refs[:3]):
        refs[3][:, j * 256 : (j + 1) * 256] = dot(x_ref[...], ref[...], TN)


def factors(at, x, sources):
    cols = [pl.BlockSpec((TOK, 256), lambda i, s, f=f: (0, f + 1 - s[0])) for _, f in sources]
    return pl.pallas_call(
        factors_body,
        grid_spec=pltpu.PrefetchScalarGridSpec(
            num_scalar_prefetch=1,
            grid=(2,),
            in_specs=[pl.BlockSpec((TOK, DM // 2), lambda i, s: (0, i))] + cols,
            out_specs=pl.BlockSpec((DM // 2, 768), lambda i, s: (i, 0)),
        ),
        out_shape=jax.ShapeDtypeStruct((DM, 768), F32),
        compiler_params=params(60),
        cost_estimate=cost(60e9, 12e6),
        name="factors",
    )(at, x, *(a for a, _ in sources))


def keep_body(at_ref, x_ref, r_ref, *refs):
    w_ref, f_ref = refs[6:]
    for j in range(3):
        cols = slice(j * 256, (j + 1) * 256)
        w_ref[:, cols] = dot(x_ref[...], refs[j][...], TN) + r_ref[:, cols]
        f_ref[:, cols] = dot(x_ref[...], refs[3 + j][...], TN).astype(BF16)


def keep(at, x, arrived, sources):
    cols = [pl.BlockSpec((TOK, 256), lambda i, s, f=f: (0, f + s[0])) for _, f in sources]
    rows = pl.BlockSpec((DM // 2, 768), lambda i, s: (i, 0))
    return pl.pallas_call(
        keep_body,
        grid_spec=pltpu.PrefetchScalarGridSpec(
            num_scalar_prefetch=1,
            grid=(2,),
            in_specs=[pl.BlockSpec((TOK, DM // 2), lambda i, s: (0, i)), rows] + cols,
            out_specs=[rows, rows],
        ),
        out_shape=[jax.ShapeDtypeStruct((DM, 768), F32), jax.ShapeDtypeStruct((DM, 768), BF16)],
        compiler_params=params(60),
        cost_estimate=cost(40e9, 16e6),
        name="keep",
    )(at, x, arrived, *(a for a, _ in sources))


def pick(axis):
    mine = lax.axis_index(axis)
    first = jnp.where(lax.axis_index("core") == 0, 1, 3)
    second = 4 - first
    return (mine, mine ^ second), (mine ^ first, mine ^ first ^ second)


def finish_body(w_hbm, a_hbm, b_hbm, sa_ref, sb_ref, kx_ref, sx_ref, ky_ref, sy_ref, w_ref, a_ref, b_ref, s_ref, sems):
    core = lax.axis_index("core")
    copies = []
    for j in range(3):
        cols = pl.ds(j * 256, 256)
        copies.append(
            (
                pltpu.make_async_copy(w_hbm.at[:, cols], w_ref.at[j], sems.at[0, j]),
                pltpu.make_async_copy(a_hbm.at[:, cols], a_ref.at[j], sems.at[1, j]),
                pltpu.make_async_copy(b_hbm.at[:, cols], b_ref.at[j], sems.at[2, j]),
            )
        )
    for pair in copies:
        for copy in pair:
            copy.start()
    for j, (kind, dims) in enumerate(((0, NT), (1, NT), (1, NN))):
        for copy in copies[j]:
            copy.wait()
        for i in range(2):
            cols = slice(i * HD, (i + 1) * HD)
            h = 2 * core + i
            far = b_ref[j, :, cols].astype(BF16)
            term = dot(a_ref[j, :, cols], sa_ref[kind, h].astype(BF16), dims)
            term += dot(far, sb_ref[kind, h].astype(BF16), dims)
            s_ref[j, :, :, :, :, cols] = (w_ref[j, :, cols] + term).reshape(8, 4, 4, 8, HD)
        lanes = slice(j * HD, (j + 1) * HD)
        kept, sent = pick("x")
        for i in range(2):
            kx_ref[:, :, i, :, lanes] = s_ref[j, :, :, kept[i], :, 0:128]
            sx_ref[:, :, i, :, lanes] = s_ref[j, :, :, sent[i], :, 0:128]
        kept, sent = pick("y")
        for i in range(2):
            ky_ref[:, i, :, :, lanes] = s_ref[j, :, kept[i], :, :, 128:256]
            sy_ref[:, i, :, :, lanes] = s_ref[j, :, sent[i], :, :, 128:256]


def finish(w, a, b, sa, sb):
    vmem = pl.BlockSpec(memory_space=pltpu.VMEM)
    hbm = pl.BlockSpec(memory_space=pltpu.HBM)
    return pl.pallas_call(
        finish_body,
        in_specs=[hbm, hbm, hbm, vmem, vmem],
        out_specs=[vmem] * 4,
        out_shape=[jax.ShapeDtypeStruct((8, 4, 2, 8, 384), F32)] * 2
        + [jax.ShapeDtypeStruct((8, 2, 4, 8, 384), F32)] * 2,
        scratch_shapes=[
            pltpu.VMEM((3, DM, 256), F32),
            pltpu.VMEM((3, DM, 256), BF16),
            pltpu.VMEM((3, DM, 256), F32),
            pltpu.VMEM((3, 8, 4, 4, 8, 256), F32),
            pltpu.SemaphoreType.DMA((3, 3)),
        ],
        compiler_params=params(49),
        cost_estimate=cost(1e9, 12e6),
        name="finish",
    )(w, a, b, sa, sb)


def inputs_body(loc_ref, qkv_ref, sg_ref, s_ref, w_ref, o_ref, d_ref):
    for h in range(H):
        before = s_ref[0, h].astype(BF16)
        after = s_ref[1, h].astype(BF16)
        parts = (
            dot(sg_ref[:, pl.ds(h * HD, HD)], before, NT),
            dot(qkv_ref[:, head(2, h)], after, NT),
            dot(qkv_ref[:, head(1, h)], after, NN),
        )
        for p, d in enumerate(parts):
            d_ref[:, head(p, h)] = (loc_ref[:, head(p, h)].astype(F32) + d).astype(BF16)
    o_ref[...] = dot(d_ref[...], w_ref[...], NT).astype(BF16)


def inputs_grad(loc, qkv, sg, states, weights):
    block = lambda cols: pl.BlockSpec((CH, cols), lambda n: (n, 0))
    return pl.pallas_call(
        inputs_body,
        grid=(NB,),
        in_specs=[
            block(3 * D),
            block(3 * D),
            block(D),
            pl.BlockSpec((2, H, HD, HD), lambda n: (0, 0, 0, 0)),
            pl.BlockSpec((DM, 3 * D), lambda n: (0, 0)),
        ],
        out_specs=block(DM),
        out_shape=jax.ShapeDtypeStruct((TOK, DM), BF16),
        scratch_shapes=[pltpu.VMEM((CH, 3 * D), BF16)],
        compiler_params=params(48),
        cost_estimate=cost(5e9, 14e6),
        name="inputs_grad",
    )(loc, qkv, sg, states, weights)


def whole_call(body, name, shapes, *args, scratch=()):
    vmem = pl.BlockSpec(memory_space=pltpu.VMEM)
    smem = pl.BlockSpec(memory_space=pltpu.SMEM)
    return pl.pallas_call(
        body,
        in_specs=[smem if a.dtype == jnp.int32 else vmem for a in args],
        out_specs=[vmem] * len(shapes),
        out_shape=[jax.ShapeDtypeStruct(s, F32) for s in shapes],
        scratch_shapes=list(scratch),
        compiler_params=params(16),
        name=name,
    )(*args)


def add1_body(k, r, ko, so):
    at = (slice(None), slice(None)) if k.shape[1] == 4 else (slice(None),)
    ko[...] = k[at + (0,)] + r[at + (0,)]
    so[...] = k[at + (1,)] + r[at + (1,)]


def add2_body(axis, k, r, ko, so):
    kept, sent = pick(axis)
    for i in range(2):
        ko[:, i] = k[:, kept[i]] + r[:, kept[i]]
        so[:, i] = k[:, sent[i]] + r[:, sent[i]]


def add3_body(k, r, ko, so):
    ko[...] = k[:, 0] + r[:, 0]
    so[...] = k[:, 1] + r[:, 1]


def add4_body(kp, rp, kq, rq, o):
    o[:, :, 0:384] = kp[...] + rp[...]
    o[:, :, 384:768] = kq[...] + rq[...]


def sum_body(v, o):
    total = v[0]
    for i in range(1, v.shape[0]):
        total = total + v[i]
    for i in range(o.shape[0]):
        o[i] = total


def place_body(v, o):
    for i in range(8):
        for p in range(6):
            at = (p % 3) * 512 + (i % 2) * 256 + (p // 3) * 128
            o[i // 2 * 8 : i // 2 * 8 + 8, at : at + 128] = v[i, :, p * 128 : (p + 1) * 128]


def exchange(value, axis, step):
    pairs = []
    for i in range(4):
        for c in range(2):
            j = i ^ ((1, 3), (3, 1))[c][step]
            pairs.append((2 * i + c, 2 * j + c))
    return lax.ppermute(value, (axis, "core"), pairs)


def shards(inputs, weights, out_grad):
    x = inputs[0]
    at = lax.axis_index("core").astype(jnp.int32)[None]

    qkv, sg, kv, qg, total = project(x, weights, out_grad[0])
    slices = lax.all_to_all(total.reshape(32, 32, HD), ("z", "y"), 0, 0, tiled=True)
    loc, given = local(at, qkv, sg, kv, qg, x)
    local_in = lax.ppermute(given, "core", SWAP)
    slices, loc = lax.optimization_barrier((slices, loc))
    scanned = scan_states(slices)
    scanned, sg, qkv, loc = lax.optimization_barrier((scanned, sg, qkv, loc))
    states = lax.all_to_all(scanned, ("z", "y"), 0, 0, tiled=True)
    given = factors(at, x, [(sg, 0), (qkv, 4), (qkv, 2)])
    factors_in = lax.ppermute(given, "core", SWAP)
    both, mine = keep(at, x, local_in, [(loc, 0), (loc, 2), (loc, 4), (sg, 0), (qkv, 4), (qkv, 2)])
    states, mine, both = lax.optimization_barrier((states, mine, both))

    states = states.reshape(2, H, HD, HD)
    states_in = lax.ppermute(states, "core", SWAP)
    kx, sx, ky, sy = finish(both, mine, factors_in, states, states_in)
    rx = exchange(sx, "x", 0)
    ry = exchange(sy, "y", 0)
    record_grad = inputs_grad(loc, qkv, sg, states, weights)
    rx, ry, record_grad = lax.optimization_barrier((rx, ry, record_grad))
    kp, sp = whole_call(add1_body, "add1x", [(8, 4, 8, 384)] * 2, kx, rx)
    rp = exchange(sp, "x", 1)
    kq, sq = whole_call(add1_body, "add1y", [(8, 4, 8, 384)] * 2, ky, ry)
    rq = exchange(sq, "y", 1)
    kp, sp = whole_call(functools.partial(add2_body, "y"), "add2x", [(8, 2, 8, 384)] * 2, kp, rp)
    rp = exchange(sp, "y", 0)
    kq, sq = whole_call(functools.partial(add2_body, "x"), "add2y", [(8, 2, 8, 384)] * 2, kq, rq)
    rq = exchange(sq, "x", 0)
    kp, sp = whole_call(add3_body, "add3x", [(8, 8, 384)] * 2, kp, rp)
    rp = exchange(sp, "y", 1)
    kq, sq = whole_call(add3_body, "add3y", [(8, 8, 384)] * 2, kq, rq)
    rq = exchange(sq, "x", 1)
    (part,) = whole_call(add4_body, "add4", [(8, 8, 768)], kp, rp, kq, rq)
    part = lax.all_to_all(part, "z", 0, 0, tiled=True)
    (own,) = whole_call(sum_body, "sum_z", [(8, 8, 768)], part)
    rows = lax.all_to_all(own, ("x", "core"), 0, 0, tiled=True)
    (proj_grad,) = whole_call(place_body, "place", [(32, 3 * D)], rows)
    return record_grad[None], proj_grad


def solution(mesh):
    fine = Mesh(mesh.devices.reshape(8, 4, 4, 2), ("z", "y", "x", "core"))
    tm, dp = ("z", "y"), ("x", "core")
    placed = (P(dp, tm, None), P(), P(dp, tm, None))
    return jax.shard_map(
        shards,
        mesh=fine,
        in_specs=placed,
        out_specs=(P(dp, tm, None), P(tm, None)),
        check_vma=False,
    )
```

```python
import functools

import jax
import jax.numpy as jnp
from jax import lax
from jax.experimental import pallas as pl
from jax.experimental.pallas import tpu as pltpu
from jax.sharding import Mesh, PartitionSpec as P

H = 4
HD = 128
CH = 256
NB = 4
D = H * HD
DM = 1024
TOK = NB * CH
F32 = jnp.float32
BF16 = jnp.bfloat16

NN = (((1,), (0,)), ((), ()))
NT = (((1,), (1,)), ((), ()))
TN = (((0,), (0,)), ((), ()))


def dot(a, b, dims):
    return lax.dot_general(a, b, dims, preferred_element_type=F32)


MIB = 1024 * 1024
SWAP = [(0, 1), (1, 0)]


def params(mib=40):
    return pltpu.CompilerParams(vmem_limit_bytes=mib * MIB)


def cost(flops, moved):
    return pl.CostEstimate(flops=int(flops), bytes_accessed=int(moved), transcendentals=0)


def head(part, h):
    return pl.ds(part * D + h * HD, HD)


def project_body(x_ref, w_ref, g_ref, qkv_ref, sg_ref, kv_ref, qg_ref, total_ref):
    n = pl.program_id(0)
    first = (lax.axis_index("z") * 4 + lax.axis_index("y")) * TOK
    qkv_ref[...] = dot(x_ref[...], w_ref[...], NN).astype(BF16)
    pos = (first + n * CH + lax.broadcasted_iota(jnp.int32, (CH, 1), 0)).astype(F32)
    factor = 1.0 / jnp.sqrt(jnp.float32(HD) * (pos + 1.0))
    sg_ref[...] = (g_ref[...].astype(F32) * factor).astype(BF16)

    @pl.when(n == 0)
    def _():
        total_ref[...] = jnp.zeros_like(total_ref)

    for h in range(H):
        kv = dot(qkv_ref[:, head(1, h)], qkv_ref[:, head(2, h)], TN)
        qg = dot(qkv_ref[:, head(0, h)], sg_ref[:, pl.ds(h * HD, HD)], TN)
        kv_ref[0, h] = kv
        qg_ref[0, h] = qg
        total_ref[0, h] += kv
        total_ref[1, h] += qg


def project(x, w, g):
    block = lambda cols: pl.BlockSpec((CH, cols), lambda n: (n, 0))
    sums = pl.BlockSpec((1, H, HD, HD), lambda n: (n, 0, 0, 0))
    return pl.pallas_call(
        project_body,
            grid=(NB,),
            in_specs=[block(DM), pl.BlockSpec((DM, 3 * D), lambda n: (0, 0)), block(D)],
            out_specs=[
                block(3 * D),
                block(D),
                sums,
                sums,
                pl.BlockSpec((2, H, HD, HD), lambda n: (0, 0, 0, 0)),
            ],
        out_shape=[
            jax.ShapeDtypeStruct((TOK, 3 * D), BF16),
            jax.ShapeDtypeStruct((TOK, D), BF16),
            jax.ShapeDtypeStruct((NB, H, HD, HD), F32),
            jax.ShapeDtypeStruct((NB, H, HD, HD), F32),
            jax.ShapeDtypeStruct((2, H, HD, HD), F32),
        ],
        compiler_params=params(60),
        name="project",
    )(x, w, g)


def scan_body(count, v_ref, o_ref):
    back = lax.axis_index("z") >= 4


    def step(t, so_far):
        i = jnp.where(back, count - 1 - t, t)
        o_ref[i] = so_far
        return so_far + v_ref[i]

    lax.fori_loop(0, count, step, jnp.zeros(v_ref.shape[1:], F32))


def scan_states(v):
    return pl.pallas_call(
        functools.partial(scan_body, v.shape[0]),
        in_specs=[pl.BlockSpec(memory_space=pltpu.VMEM)],
        out_specs=pl.BlockSpec(memory_space=pltpu.VMEM),
        out_shape=jax.ShapeDtypeStruct(v.shape, F32),
        compiler_params=params(4),
        name="scan_states",
    )(v)


def local_body(at_ref, qkv_ref, sg_ref, kv_ref, qg_ref, x_hbm, loc_ref, give_ref, from_ref, x_ref, sem):
    n = pl.program_id(0)
    copy = pltpu.make_async_copy(x_hbm, x_ref, sem)
    theirs = pl.multiple_of((1 - at_ref[0]) * 256, 256)

    @pl.when(n == 0)
    def _():
        copy.start()

    @pl.when(n < NB)
    def _():
        keep = lax.broadcasted_iota(jnp.int32, (CH, CH), 0) >= lax.broadcasted_iota(jnp.int32, (CH, CH), 1)
        for h in range(H):
            q, k, v = (qkv_ref[:, head(p, h)] for p in range(3))
            g = sg_ref[:, pl.ds(h * HD, HD)]
            before = jnp.zeros((HD, HD), F32)
            after = jnp.zeros((HD, HD), F32)
            for m in range(NB):
                before = before + jnp.where(m < n, kv_ref[m, h], 0.0)
                after = after + jnp.where(m > n, qg_ref[m, h], 0.0)
            before = before.astype(BF16)
            after = after.astype(BF16)
            mvg = jnp.where(keep, dot(g, v, NT), 0.0).astype(BF16)
            mqk = jnp.where(keep, dot(q, k, NT), 0.0).astype(BF16)
            dq = dot(mvg, k, NN) + dot(g, before, NT)
            dk = dot(mvg, q, TN) + dot(v, after, NT)
            dv = dot(mqk, g, TN) + dot(k, after, NN)
            for p, d in enumerate((dq, dk, dv)):
                loc_ref[:, head(p, h)] = d.astype(BF16)
        rows = pl.ds(pl.multiple_of(n * CH, CH), CH)
        for p in range(3):
            from_ref[rows, p * 256 : (p + 1) * 256] = loc_ref[:, pl.ds(p * D + theirs, 256)]

    @pl.when(n == NB)
    def _():
        copy.wait()

    @pl.when(n >= NB)
    def _():
        half = pl.ds(pl.multiple_of((n - NB) * (DM // 2), DM // 2), DM // 2)
        give_ref[...] = dot(x_ref[:, half], from_ref[...], TN)


def local(at, qkv, sg, kv, qg, x):
    first = lambda n: jnp.minimum(n, NB - 1)
    last = lambda n: jnp.maximum(n - NB, 0)
    block = lambda cols: pl.BlockSpec((CH, cols), lambda n, s: (first(n), 0))
    sums = pl.BlockSpec((NB, H, HD, HD), lambda n, s: (0, 0, 0, 0))
    return pl.pallas_call(
        local_body,
        grid_spec=pltpu.PrefetchScalarGridSpec(
            num_scalar_prefetch=1,
            grid=(NB + 2,),
            in_specs=[
                block(3 * D),
                block(D),
                sums,
                sums,
                pl.BlockSpec(memory_space=pltpu.HBM),
            ],
            out_specs=[block(3 * D), pl.BlockSpec((DM // 2, 768), lambda n, s: (last(n), 0))],
            scratch_shapes=[
                pltpu.VMEM((TOK, 768), BF16),
                pltpu.VMEM((TOK, DM), BF16),
                pltpu.SemaphoreType.DMA,
            ],
        ),
        out_shape=[
            jax.ShapeDtypeStruct((TOK, 3 * D), BF16),
            jax.ShapeDtypeStruct((DM, 768), F32),
        ],
        compiler_params=params(60),
        cost_estimate=cost(8e9, 24e6),
        name="local",
    )(at, qkv, sg, kv, qg, x)


def factors_body(at_ref, x_ref, *refs):
    for j, ref in enumerate(refs[:3]):
        refs[3][:, j * 256 : (j + 1) * 256] = dot(x_ref[...], ref[...], TN)


def factors(at, x, sources):
    cols = [pl.BlockSpec((TOK, 256), lambda i, s, f=f: (0, f + 1 - s[0])) for _, f in sources]
    return pl.pallas_call(
        factors_body,
        grid_spec=pltpu.PrefetchScalarGridSpec(
            num_scalar_prefetch=1,
            grid=(2,),
            in_specs=[pl.BlockSpec((TOK, DM // 2), lambda i, s: (0, i))] + cols,
            out_specs=pl.BlockSpec((DM // 2, 768), lambda i, s: (i, 0)),
        ),
        out_shape=jax.ShapeDtypeStruct((DM, 768), F32),
        compiler_params=params(60),
        cost_estimate=cost(60e9, 12e6),
        name="factors",
    )(at, x, *(a for a, _ in sources))


def keep_body(at_ref, x_ref, r_ref, *refs):
    w_ref, f_ref = refs[6:]
    for j in range(3):
        cols = slice(j * 256, (j + 1) * 256)
        w_ref[:, cols] = dot(x_ref[...], refs[j][...], TN) + r_ref[:, cols]
        f_ref[:, cols] = dot(x_ref[...], refs[3 + j][...], TN).astype(BF16)


def keep(at, x, arrived, sources):
    cols = [pl.BlockSpec((TOK, 256), lambda i, s, f=f: (0, f + s[0])) for _, f in sources]
    rows = pl.BlockSpec((DM // 2, 768), lambda i, s: (i, 0))
    return pl.pallas_call(
        keep_body,
        grid_spec=pltpu.PrefetchScalarGridSpec(
            num_scalar_prefetch=1,
            grid=(2,),
            in_specs=[pl.BlockSpec((TOK, DM // 2), lambda i, s: (0, i)), rows] + cols,
            out_specs=[rows, rows],
        ),
        out_shape=[jax.ShapeDtypeStruct((DM, 768), F32), jax.ShapeDtypeStruct((DM, 768), BF16)],
        compiler_params=params(60),
        cost_estimate=cost(40e9, 16e6),
        name="keep",
    )(at, x, arrived, *(a for a, _ in sources))


def pick(axis):
    mine = lax.axis_index(axis)
    first = jnp.where(lax.axis_index("core") == 0, 1, 3)
    second = 4 - first
    return (mine, mine ^ second), (mine ^ first, mine ^ first ^ second)


def own_body(w_hbm, a_hbm, b_hbm, s_ref, o_ref, far_ref, w_ref, a_ref, b_ref, sems):
    core = lax.axis_index("core")
    copies = []
    for j in range(3):
        cols = pl.ds(j * 256, 256)
        copies.append(
            (
                pltpu.make_async_copy(w_hbm.at[:, cols], w_ref.at[j], sems.at[0, j]),
                pltpu.make_async_copy(a_hbm.at[:, cols], a_ref.at[j], sems.at[1, j]),
                pltpu.make_async_copy(b_hbm.at[:, cols], b_ref.at[j], sems.at[2, j]),
            )
        )
    for group in copies:
        for copy in group:
            copy.start()
    for j, (kind, dims) in enumerate(((0, NT), (1, NT), (1, NN))):
        for copy in copies[j]:
            copy.wait()
        for i in range(2):
            cols = slice(i * HD, (i + 1) * HD)
            term = dot(a_ref[j, :, cols], s_ref[kind, 2 * core + i].astype(BF16), dims)
            o_ref[j, :, cols] = w_ref[j, :, cols] + term
        far_ref[j] = b_ref[j].astype(BF16)


def own_states(w, a, b, states):
    vmem = pl.BlockSpec(memory_space=pltpu.VMEM)
    hbm = pl.BlockSpec(memory_space=pltpu.HBM)
    return pl.pallas_call(
        own_body,
        in_specs=[hbm, hbm, hbm, vmem],
        out_specs=[vmem, vmem],
        out_shape=[
            jax.ShapeDtypeStruct((3, DM, 256), F32),
            jax.ShapeDtypeStruct((3, DM, 256), BF16),
        ],
        scratch_shapes=[
            pltpu.VMEM((3, DM, 256), F32),
            pltpu.VMEM((3, DM, 256), BF16),
            pltpu.VMEM((3, DM, 256), F32),
            pltpu.SemaphoreType.DMA((3, 3)),
        ],
        compiler_params=params(47),
        cost_estimate=cost(5e9, 12e6),
        name="own_states",
    )(w, a, b, states)


def finish_body(w_ref, b_ref, s_ref, kx_ref, sx_ref, ky_ref, sy_ref, t_ref):
    core = lax.axis_index("core")
    for j, (kind, dims) in enumerate(((0, NT), (1, NT), (1, NN))):
        for i in range(2):
            cols = slice(i * HD, (i + 1) * HD)
            term = dot(b_ref[j, :, cols], s_ref[kind, 2 * core + i].astype(BF16), dims)
            t_ref[j, :, :, :, :, cols] = (w_ref[j, :, cols] + term).reshape(8, 4, 4, 8, HD)
        lanes = slice(j * HD, (j + 1) * HD)
        kept, sent = pick("x")
        for i in range(2):
            kx_ref[:, :, i, :, lanes] = t_ref[j, :, :, kept[i], :, 0:128]
            sx_ref[:, :, i, :, lanes] = t_ref[j, :, :, sent[i], :, 0:128]
        kept, sent = pick("y")
        for i in range(2):
            ky_ref[:, i, :, :, lanes] = t_ref[j, :, kept[i], :, :, 128:256]
            sy_ref[:, i, :, :, lanes] = t_ref[j, :, sent[i], :, :, 128:256]


def finish(w, b, states):
    vmem = pl.BlockSpec(memory_space=pltpu.VMEM)
    return pl.pallas_call(
        finish_body,
        in_specs=[vmem] * 3,
        out_specs=[vmem] * 4,
        out_shape=[jax.ShapeDtypeStruct((8, 4, 2, 8, 384), F32)] * 2
        + [jax.ShapeDtypeStruct((8, 2, 4, 8, 384), F32)] * 2,
        scratch_shapes=[pltpu.VMEM((3, 8, 4, 4, 8, 256), F32)],
        compiler_params=params(44),
        cost_estimate=cost(1e9, 12e6),
        name="finish",
    )(w, b, states)


def inputs_body(loc_ref, qkv_ref, sg_ref, s_ref, w_ref, o_ref, d_ref):
    for h in range(H):
        before = s_ref[0, h].astype(BF16)
        after = s_ref[1, h].astype(BF16)
        parts = (
            dot(sg_ref[:, pl.ds(h * HD, HD)], before, NT),
            dot(qkv_ref[:, head(2, h)], after, NT),
            dot(qkv_ref[:, head(1, h)], after, NN),
        )
        for p, d in enumerate(parts):
            d_ref[:, head(p, h)] = (loc_ref[:, head(p, h)].astype(F32) + d).astype(BF16)
    o_ref[...] = dot(d_ref[...], w_ref[...], NT).astype(BF16)


def inputs_grad(loc, qkv, sg, states, weights):
    block = lambda cols: pl.BlockSpec((CH, cols), lambda n: (n, 0))
    return pl.pallas_call(
        inputs_body,
        grid=(NB,),
        in_specs=[
            block(3 * D),
            block(3 * D),
            block(D),
            pl.BlockSpec((2, H, HD, HD), lambda n: (0, 0, 0, 0)),
            pl.BlockSpec((DM, 3 * D), lambda n: (0, 0)),
        ],
        out_specs=block(DM),
        out_shape=jax.ShapeDtypeStruct((TOK, DM), BF16),
        scratch_shapes=[pltpu.VMEM((CH, 3 * D), BF16)],
        compiler_params=params(50),
        cost_estimate=cost(5e9, 14e6),
        name="inputs_grad",
    )(loc, qkv, sg, states, weights)


def whole_call(body, name, shapes, *args, scratch=()):
    vmem = pl.BlockSpec(memory_space=pltpu.VMEM)
    smem = pl.BlockSpec(memory_space=pltpu.SMEM)
    return pl.pallas_call(
        body,
        in_specs=[smem if a.dtype == jnp.int32 else vmem for a in args],
        out_specs=[vmem] * len(shapes),
        out_shape=[jax.ShapeDtypeStruct(s, F32) for s in shapes],
        scratch_shapes=list(scratch),
        compiler_params=params(16),
        name=name,
    )(*args)


def add1_body(k, r, ko, so):
    at = (slice(None), slice(None)) if k.shape[1] == 4 else (slice(None),)
    ko[...] = k[at + (0,)] + r[at + (0,)]
    so[...] = k[at + (1,)] + r[at + (1,)]


def add2_body(axis, k, r, ko, so):
    kept, sent = pick(axis)
    for i in range(2):
        ko[:, i] = k[:, kept[i]] + r[:, kept[i]]
        so[:, i] = k[:, sent[i]] + r[:, sent[i]]


def add3_body(k, r, ko, so):
    ko[...] = k[:, 0] + r[:, 0]
    so[...] = k[:, 1] + r[:, 1]


def add4_body(kp, rp, kq, rq, o):
    o[:, :, 0:384] = kp[...] + rp[...]
    o[:, :, 384:768] = kq[...] + rq[...]


def sum_body(v, o):
    total = v[0]
    for i in range(1, v.shape[0]):
        total = total + v[i]
    for i in range(o.shape[0]):
        o[i] = total


def place_body(v, o):
    for i in range(8):
        for p in range(6):
            at = (p % 3) * 512 + (i % 2) * 256 + (p // 3) * 128
            o[i // 2 * 8 : i // 2 * 8 + 8, at : at + 128] = v[i, :, p * 128 : (p + 1) * 128]


def exchange(value, axis, step):
    pairs = []
    for i in range(4):
        for c in range(2):
            j = i ^ ((1, 3), (3, 1))[c][step]
            pairs.append((2 * i + c, 2 * j + c))
    return lax.ppermute(value, (axis, "core"), pairs)


def shards(inputs, weights, out_grad):
    x = inputs[0]
    at = lax.axis_index("core").astype(jnp.int32)[None]

    qkv, sg, kv, qg, total = project(x, weights, out_grad[0])
    slices = lax.all_to_all(total.reshape(32, 32, HD), ("z", "y"), 0, 0, tiled=True)
    loc, given = local(at, qkv, sg, kv, qg, x)
    local_in = lax.ppermute(given, "core", SWAP)
    slices, loc = lax.optimization_barrier((slices, loc))
    scanned = scan_states(slices)
    scanned, sg, qkv, loc = lax.optimization_barrier((scanned, sg, qkv, loc))
    states = lax.all_to_all(scanned, ("z", "y"), 0, 0, tiled=True)
    given = factors(at, x, [(sg, 0), (qkv, 4), (qkv, 2)])
    factors_in = lax.ppermute(given, "core", SWAP)
    both, mine = keep(at, x, local_in, [(loc, 0), (loc, 2), (loc, 4), (sg, 0), (qkv, 4), (qkv, 2)])
    states, mine, both = lax.optimization_barrier((states, mine, both))

    states = states.reshape(2, H, HD, HD)
    states_in = lax.ppermute(states, "core", SWAP)
    both, far = own_states(both, mine, factors_in, states)
    kx, sx, ky, sy = finish(both, far, states_in)
    rx = exchange(sx, "x", 0)
    ry = exchange(sy, "y", 0)
    record_grad = inputs_grad(loc, qkv, sg, states, weights)
    rx, ry, record_grad = lax.optimization_barrier((rx, ry, record_grad))
    kp, sp = whole_call(add1_body, "add1x", [(8, 4, 8, 384)] * 2, kx, rx)
    rp = exchange(sp, "x", 1)
    kq, sq = whole_call(add1_body, "add1y", [(8, 4, 8, 384)] * 2, ky, ry)
    rq = exchange(sq, "y", 1)
    kp, sp = whole_call(functools.partial(add2_body, "y"), "add2x", [(8, 2, 8, 384)] * 2, kp, rp)
    rp = exchange(sp, "y", 0)
    kq, sq = whole_call(functools.partial(add2_body, "x"), "add2y", [(8, 2, 8, 384)] * 2, kq, rq)
    rq = exchange(sq, "x", 0)
    kp, sp = whole_call(add3_body, "add3x", [(8, 8, 384)] * 2, kp, rp)
    rp = exchange(sp, "y", 1)
    kq, sq = whole_call(add3_body, "add3y", [(8, 8, 384)] * 2, kq, rq)
    rq = exchange(sq, "x", 1)
    (part,) = whole_call(add4_body, "add4", [(8, 8, 768)], kp, rp, kq, rq)
    part = lax.all_to_all(part, "z", 0, 0, tiled=True)
    (own,) = whole_call(sum_body, "sum_z", [(8, 8, 768)], part)
    rows = lax.all_to_all(own, ("x", "core"), 0, 0, tiled=True)
    (proj_grad,) = whole_call(place_body, "place", [(32, 3 * D)], rows)
    return record_grad[None], proj_grad


def solution(mesh):
    fine = Mesh(mesh.devices.reshape(8, 4, 4, 2), ("z", "y", "x", "core"))
    tm, dp = ("z", "y"), ("x", "core")
    placed = (P(dp, tm, None), P(), P(dp, tm, None))
    return jax.shard_map(
        shards,
        mesh=fine,
        in_specs=placed,
        out_specs=(P(dp, tm, None), P(tm, None)),
        check_vma=False,
    )
```

```python
import functools

import jax
import jax.numpy as jnp
from jax import lax
from jax.experimental import pallas as pl
from jax.experimental.pallas import tpu as pltpu
from jax.sharding import Mesh, PartitionSpec as P

H = 4
HD = 128
CH = 256
NB = 4
D = H * HD
DM = 1024
TOK = NB * CH
F32 = jnp.float32
BF16 = jnp.bfloat16

NN = (((1,), (0,)), ((), ()))
NT = (((1,), (1,)), ((), ()))
TN = (((0,), (0,)), ((), ()))


def dot(a, b, dims):
    return lax.dot_general(a, b, dims, preferred_element_type=F32)


MIB = 1024 * 1024
SWAP = [(0, 1), (1, 0)]


def params(mib=40):
    return pltpu.CompilerParams(vmem_limit_bytes=mib * MIB)


def cost(flops, moved):
    return pl.CostEstimate(flops=int(flops), bytes_accessed=int(moved), transcendentals=0)


def head(part, h):
    return pl.ds(part * D + h * HD, HD)


def project_body(x_ref, w_ref, g_ref, qkv_ref, sg_ref, kv_ref, qg_ref, total_ref):
    n = pl.program_id(0)
    first = (lax.axis_index("z") * 4 + lax.axis_index("y")) * TOK
    qkv_ref[...] = dot(x_ref[...], w_ref[...], NN).astype(BF16)
    pos = (first + n * CH + lax.broadcasted_iota(jnp.int32, (CH, 1), 0)).astype(F32)
    factor = 1.0 / jnp.sqrt(jnp.float32(HD) * (pos + 1.0))
    sg_ref[...] = (g_ref[...].astype(F32) * factor).astype(BF16)

    @pl.when(n == 0)
    def _():
        total_ref[...] = jnp.zeros_like(total_ref)

    for h in range(H):
        kv = dot(qkv_ref[:, head(1, h)], qkv_ref[:, head(2, h)], TN)
        qg = dot(qkv_ref[:, head(0, h)], sg_ref[:, pl.ds(h * HD, HD)], TN)
        kv_ref[0, h] = kv
        qg_ref[0, h] = qg
        total_ref[0, h] += kv
        total_ref[1, h] += qg


def project(x, w, g):
    block = lambda cols: pl.BlockSpec((CH, cols), lambda n: (n, 0))
    sums = pl.BlockSpec((1, H, HD, HD), lambda n: (n, 0, 0, 0))
    return pl.pallas_call(
        project_body,
            grid=(NB,),
            in_specs=[block(DM), pl.BlockSpec((DM, 3 * D), lambda n: (0, 0)), block(D)],
            out_specs=[
                block(3 * D),
                block(D),
                sums,
                sums,
                pl.BlockSpec((2, H, HD, HD), lambda n: (0, 0, 0, 0)),
            ],
        out_shape=[
            jax.ShapeDtypeStruct((TOK, 3 * D), BF16),
            jax.ShapeDtypeStruct((TOK, D), BF16),
            jax.ShapeDtypeStruct((NB, H, HD, HD), F32),
            jax.ShapeDtypeStruct((NB, H, HD, HD), F32),
            jax.ShapeDtypeStruct((2, H, HD, HD), F32),
        ],
        compiler_params=params(60),
        name="project",
    )(x, w, g)


def scan_body(count, v_ref, o_ref):
    back = lax.axis_index("z") >= 4


    def step(t, so_far):
        i = jnp.where(back, count - 1 - t, t)
        o_ref[i] = so_far
        return so_far + v_ref[i]

    lax.fori_loop(0, count, step, jnp.zeros(v_ref.shape[1:], F32))


def scan_states(v):
    return pl.pallas_call(
        functools.partial(scan_body, v.shape[0]),
        in_specs=[pl.BlockSpec(memory_space=pltpu.VMEM)],
        out_specs=pl.BlockSpec(memory_space=pltpu.VMEM),
        out_shape=jax.ShapeDtypeStruct(v.shape, F32),
        compiler_params=params(4),
        name="scan_states",
    )(v)


def local_body(at_ref, qkv_ref, sg_ref, kv_ref, qg_ref, x_hbm, loc_ref, give_ref, from_ref, x_ref, sem):
    n = pl.program_id(0)
    copy = pltpu.make_async_copy(x_hbm, x_ref, sem)
    theirs = pl.multiple_of((1 - at_ref[0]) * 256, 256)

    @pl.when(n == 0)
    def _():
        copy.start()

    @pl.when(n < NB)
    def _():
        keep = lax.broadcasted_iota(jnp.int32, (CH, CH), 0) >= lax.broadcasted_iota(jnp.int32, (CH, CH), 1)
        for h in range(H):
            q, k, v = (qkv_ref[:, head(p, h)] for p in range(3))
            g = sg_ref[:, pl.ds(h * HD, HD)]
            before = jnp.zeros((HD, HD), F32)
            after = jnp.zeros((HD, HD), F32)
            for m in range(NB):
                before = before + jnp.where(m < n, kv_ref[m, h], 0.0)
                after = after + jnp.where(m > n, qg_ref[m, h], 0.0)
            before = before.astype(BF16)
            after = after.astype(BF16)
            mvg = jnp.where(keep, dot(g, v, NT), 0.0).astype(BF16)
            mqk = jnp.where(keep, dot(q, k, NT), 0.0).astype(BF16)
            dq = dot(mvg, k, NN) + dot(g, before, NT)
            dk = dot(mvg, q, TN) + dot(v, after, NT)
            dv = dot(mqk, g, TN) + dot(k, after, NN)
            for p, d in enumerate((dq, dk, dv)):
                loc_ref[:, head(p, h)] = d.astype(BF16)
        rows = pl.ds(pl.multiple_of(n * CH, CH), CH)
        for p in range(3):
            from_ref[rows, p * 256 : (p + 1) * 256] = loc_ref[:, pl.ds(p * D + theirs, 256)]

    @pl.when(n == NB)
    def _():
        copy.wait()

    @pl.when(n >= NB)
    def _():
        half = pl.ds(pl.multiple_of((n - NB) * (DM // 2), DM // 2), DM // 2)
        give_ref[...] = dot(x_ref[:, half], from_ref[...], TN)


def local(at, qkv, sg, kv, qg, x):
    first = lambda n: jnp.minimum(n, NB - 1)
    last = lambda n: jnp.maximum(n - NB, 0)
    block = lambda cols: pl.BlockSpec((CH, cols), lambda n, s: (first(n), 0))
    sums = pl.BlockSpec((NB, H, HD, HD), lambda n, s: (0, 0, 0, 0))
    return pl.pallas_call(
        local_body,
        grid_spec=pltpu.PrefetchScalarGridSpec(
            num_scalar_prefetch=1,
            grid=(NB + 2,),
            in_specs=[
                block(3 * D),
                block(D),
                sums,
                sums,
                pl.BlockSpec(memory_space=pltpu.HBM),
            ],
            out_specs=[block(3 * D), pl.BlockSpec((DM // 2, 768), lambda n, s: (last(n), 0))],
            scratch_shapes=[
                pltpu.VMEM((TOK, 768), BF16),
                pltpu.VMEM((TOK, DM), BF16),
                pltpu.SemaphoreType.DMA,
            ],
        ),
        out_shape=[
            jax.ShapeDtypeStruct((TOK, 3 * D), BF16),
            jax.ShapeDtypeStruct((DM, 768), F32),
        ],
        compiler_params=params(60),
        cost_estimate=cost(8e9, 24e6),
        name="local",
    )(at, qkv, sg, kv, qg, x)


def factors_body(at_ref, x_ref, *refs):
    for j, ref in enumerate(refs[:3]):
        refs[3][:, j * 256 : (j + 1) * 256] = dot(x_ref[...], ref[...], TN)


def factors(at, x, sources):
    cols = [pl.BlockSpec((TOK, 256), lambda i, s, f=f: (0, f + 1 - s[0])) for _, f in sources]
    return pl.pallas_call(
        factors_body,
        grid_spec=pltpu.PrefetchScalarGridSpec(
            num_scalar_prefetch=1,
            grid=(2,),
            in_specs=[pl.BlockSpec((TOK, DM // 2), lambda i, s: (0, i))] + cols,
            out_specs=pl.BlockSpec((DM // 2, 768), lambda i, s: (i, 0)),
        ),
        out_shape=jax.ShapeDtypeStruct((DM, 768), F32),
        compiler_params=params(60),
        cost_estimate=cost(60e9, 12e6),
        name="factors",
    )(at, x, *(a for a, _ in sources))


def keep_body(at_ref, x_ref, r_ref, *refs):
    w_ref, f_ref = refs[6:]
    for j in range(3):
        cols = slice(j * 256, (j + 1) * 256)
        w_ref[:, cols] = dot(x_ref[...], refs[j][...], TN) + r_ref[:, cols]
        factor = dot(x_ref[...], refs[3 + j][...], TN)
        high = factor.astype(BF16)
        f_ref[0, :, cols] = high
        f_ref[1, :, cols] = (factor - high.astype(F32)).astype(BF16)


def keep(at, x, arrived, sources):
    cols = [pl.BlockSpec((TOK, 256), lambda i, s, f=f: (0, f + s[0])) for _, f in sources]
    rows = pl.BlockSpec((DM // 2, 768), lambda i, s: (i, 0))
    return pl.pallas_call(
        keep_body,
        grid_spec=pltpu.PrefetchScalarGridSpec(
            num_scalar_prefetch=1,
            grid=(2,),
            in_specs=[pl.BlockSpec((TOK, DM // 2), lambda i, s: (0, i)), rows] + cols,
            out_specs=[rows, pl.BlockSpec((2, DM // 2, 768), lambda i, s: (0, i, 0))],
        ),
        out_shape=[jax.ShapeDtypeStruct((DM, 768), F32), jax.ShapeDtypeStruct((2, DM, 768), BF16)],
        compiler_params=params(60),
        cost_estimate=cost(40e9, 16e6),
        name="keep",
    )(at, x, arrived, *(a for a, _ in sources))


def pick(axis):
    mine = lax.axis_index(axis)
    first = jnp.where(lax.axis_index("core") == 0, 1, 3)
    second = 4 - first
    return (mine, mine ^ second), (mine ^ first, mine ^ first ^ second)


def own_body(w_hbm, a_hbm, b_hbm, s_ref, o_ref, far_ref, w_ref, a_ref, b_ref, sems):
    core = lax.axis_index("core")
    copies = []
    for j in range(3):
        cols = pl.ds(j * 256, 256)
        copies.append(
            (
                pltpu.make_async_copy(w_hbm.at[:, cols], w_ref.at[j], sems.at[0, j]),
                pltpu.make_async_copy(a_hbm.at[:, :, cols], a_ref.at[j], sems.at[1, j]),
                pltpu.make_async_copy(b_hbm.at[:, cols], b_ref.at[j], sems.at[2, j]),
            )
        )
    for group in copies:
        for copy in group:
            copy.start()
    for j, (kind, dims) in enumerate(((0, NT), (1, NT), (1, NN))):
        for copy in copies[j]:
            copy.wait()
        for i in range(2):
            cols = slice(i * HD, (i + 1) * HD)
            state = s_ref[kind, 2 * core + i].astype(BF16)
            term = dot(a_ref[j, 0, :, cols], state, dims) + dot(a_ref[j, 1, :, cols], state, dims)
            o_ref[j, :, cols] = w_ref[j, :, cols] + term
        far_ref[j] = b_ref[j].astype(BF16)


def own_states(w, a, b, states):
    vmem = pl.BlockSpec(memory_space=pltpu.VMEM)
    hbm = pl.BlockSpec(memory_space=pltpu.HBM)
    return pl.pallas_call(
        own_body,
        in_specs=[hbm, hbm, hbm, vmem],
        out_specs=[vmem, vmem],
        out_shape=[
            jax.ShapeDtypeStruct((3, DM, 256), F32),
            jax.ShapeDtypeStruct((3, DM, 256), BF16),
        ],
        scratch_shapes=[
            pltpu.VMEM((3, DM, 256), F32),
            pltpu.VMEM((3, 2, DM, 256), BF16),
            pltpu.VMEM((3, DM, 256), F32),
            pltpu.SemaphoreType.DMA((3, 3)),
        ],
        compiler_params=params(47),
        cost_estimate=cost(5e9, 12e6),
        name="own_states",
    )(w, a, b, states)


def finish_body(w_ref, b_ref, s_ref, kx_ref, sx_ref, ky_ref, sy_ref, t_ref):
    core = lax.axis_index("core")
    for j, (kind, dims) in enumerate(((0, NT), (1, NT), (1, NN))):
        for i in range(2):
            cols = slice(i * HD, (i + 1) * HD)
            term = dot(b_ref[j, :, cols], s_ref[kind, 2 * core + i].astype(BF16), dims)
            t_ref[j, :, :, :, :, cols] = (w_ref[j, :, cols] + term).reshape(8, 4, 4, 8, HD)
        lanes = slice(j * HD, (j + 1) * HD)
        kept, sent = pick("x")
        for i in range(2):
            kx_ref[:, :, i, :, lanes] = t_ref[j, :, :, kept[i], :, 0:128]
            sx_ref[:, :, i, :, lanes] = t_ref[j, :, :, sent[i], :, 0:128]
        kept, sent = pick("y")
        for i in range(2):
            ky_ref[:, i, :, :, lanes] = t_ref[j, :, kept[i], :, :, 128:256]
            sy_ref[:, i, :, :, lanes] = t_ref[j, :, sent[i], :, :, 128:256]


def finish(w, b, states):
    vmem = pl.BlockSpec(memory_space=pltpu.VMEM)
    return pl.pallas_call(
        finish_body,
        in_specs=[vmem] * 3,
        out_specs=[vmem] * 4,
        out_shape=[jax.ShapeDtypeStruct((8, 4, 2, 8, 384), F32)] * 2
        + [jax.ShapeDtypeStruct((8, 2, 4, 8, 384), F32)] * 2,
        scratch_shapes=[pltpu.VMEM((3, 8, 4, 4, 8, 256), F32)],
        compiler_params=params(44),
        cost_estimate=cost(1e9, 12e6),
        name="finish",
    )(w, b, states)


def inputs_body(loc_ref, qkv_ref, sg_ref, s_ref, w_ref, o_ref, d_ref):
    for h in range(H):
        before = s_ref[0, h].astype(BF16)
        after = s_ref[1, h].astype(BF16)
        parts = (
            dot(sg_ref[:, pl.ds(h * HD, HD)], before, NT),
            dot(qkv_ref[:, head(2, h)], after, NT),
            dot(qkv_ref[:, head(1, h)], after, NN),
        )
        for p, d in enumerate(parts):
            d_ref[:, head(p, h)] = (loc_ref[:, head(p, h)].astype(F32) + d).astype(BF16)
    o_ref[...] = dot(d_ref[...], w_ref[...], NT).astype(BF16)


def inputs_grad(loc, qkv, sg, states, weights):
    block = lambda cols: pl.BlockSpec((CH, cols), lambda n: (n, 0))
    return pl.pallas_call(
        inputs_body,
        grid=(NB,),
        in_specs=[
            block(3 * D),
            block(3 * D),
            block(D),
            pl.BlockSpec((2, H, HD, HD), lambda n: (0, 0, 0, 0)),
            pl.BlockSpec((DM, 3 * D), lambda n: (0, 0)),
        ],
        out_specs=block(DM),
        out_shape=jax.ShapeDtypeStruct((TOK, DM), BF16),
        scratch_shapes=[pltpu.VMEM((CH, 3 * D), BF16)],
        compiler_params=params(50),
        cost_estimate=cost(5e9, 14e6),
        name="inputs_grad",
    )(loc, qkv, sg, states, weights)


def whole_call(body, name, shapes, *args, scratch=()):
    vmem = pl.BlockSpec(memory_space=pltpu.VMEM)
    smem = pl.BlockSpec(memory_space=pltpu.SMEM)
    return pl.pallas_call(
        body,
        in_specs=[smem if a.dtype == jnp.int32 else vmem for a in args],
        out_specs=[vmem] * len(shapes),
        out_shape=[jax.ShapeDtypeStruct(s, F32) for s in shapes],
        scratch_shapes=list(scratch),
        compiler_params=params(16),
        name=name,
    )(*args)


def add1_body(k, r, ko, so):
    at = (slice(None), slice(None)) if k.shape[1] == 4 else (slice(None),)
    ko[...] = k[at + (0,)] + r[at + (0,)]
    so[...] = k[at + (1,)] + r[at + (1,)]


def add2_body(axis, k, r, ko, so):
    kept, sent = pick(axis)
    for i in range(2):
        ko[:, i] = k[:, kept[i]] + r[:, kept[i]]
        so[:, i] = k[:, sent[i]] + r[:, sent[i]]


def add3_body(k, r, ko, so):
    ko[...] = k[:, 0] + r[:, 0]
    so[...] = k[:, 1] + r[:, 1]


def add4_body(kp, rp, kq, rq, o):
    o[:, :, 0:384] = kp[...] + rp[...]
    o[:, :, 384:768] = kq[...] + rq[...]


def sum_body(v, o):
    total = v[0]
    for i in range(1, v.shape[0]):
        total = total + v[i]
    for i in range(o.shape[0]):
        o[i] = total


def place_body(v, o):
    for i in range(8):
        for p in range(6):
            at = (p % 3) * 512 + (i % 2) * 256 + (p // 3) * 128
            o[i // 2 * 8 : i // 2 * 8 + 8, at : at + 128] = v[i, :, p * 128 : (p + 1) * 128]


def exchange(value, axis, step):
    pairs = []
    for i in range(4):
        for c in range(2):
            j = i ^ ((1, 3), (3, 1))[c][step]
            pairs.append((2 * i + c, 2 * j + c))
    return lax.ppermute(value, (axis, "core"), pairs)


def shards(inputs, weights, out_grad):
    x = inputs[0]
    at = lax.axis_index("core").astype(jnp.int32)[None]

    qkv, sg, kv, qg, total = project(x, weights, out_grad[0])
    slices = lax.all_to_all(total.reshape(32, 32, HD), ("z", "y"), 0, 0, tiled=True)
    loc, given = local(at, qkv, sg, kv, qg, x)
    local_in = lax.ppermute(given, "core", SWAP)
    slices, loc = lax.optimization_barrier((slices, loc))
    scanned = scan_states(slices)
    scanned, sg, qkv, loc = lax.optimization_barrier((scanned, sg, qkv, loc))
    states = lax.all_to_all(scanned, ("z", "y"), 0, 0, tiled=True)
    given = factors(at, x, [(sg, 0), (qkv, 4), (qkv, 2)])
    factors_in = lax.ppermute(given, "core", SWAP)
    both, mine = keep(at, x, local_in, [(loc, 0), (loc, 2), (loc, 4), (sg, 0), (qkv, 4), (qkv, 2)])
    states, mine, both = lax.optimization_barrier((states, mine, both))

    states = states.reshape(2, H, HD, HD)
    states_in = lax.ppermute(states, "core", SWAP)
    both, far = own_states(both, mine, factors_in, states)
    kx, sx, ky, sy = finish(both, far, states_in)
    rx = exchange(sx, "x", 0)
    ry = exchange(sy, "y", 0)
    record_grad = inputs_grad(loc, qkv, sg, states, weights)
    rx, ry, record_grad = lax.optimization_barrier((rx, ry, record_grad))
    kp, sp = whole_call(add1_body, "add1x", [(8, 4, 8, 384)] * 2, kx, rx)
    rp = exchange(sp, "x", 1)
    kq, sq = whole_call(add1_body, "add1y", [(8, 4, 8, 384)] * 2, ky, ry)
    rq = exchange(sq, "y", 1)
    kp, sp = whole_call(functools.partial(add2_body, "y"), "add2x", [(8, 2, 8, 384)] * 2, kp, rp)
    rp = exchange(sp, "y", 0)
    kq, sq = whole_call(functools.partial(add2_body, "x"), "add2y", [(8, 2, 8, 384)] * 2, kq, rq)
    rq = exchange(sq, "x", 0)
    kp, sp = whole_call(add3_body, "add3x", [(8, 8, 384)] * 2, kp, rp)
    rp = exchange(sp, "y", 1)
    kq, sq = whole_call(add3_body, "add3y", [(8, 8, 384)] * 2, kq, rq)
    rq = exchange(sq, "x", 1)
    (part,) = whole_call(add4_body, "add4", [(8, 8, 768)], kp, rp, kq, rq)
    part = lax.all_to_all(part, "z", 0, 0, tiled=True)
    (own,) = whole_call(sum_body, "sum_z", [(8, 8, 768)], part)
    rows = lax.all_to_all(own, ("x", "core"), 0, 0, tiled=True)
    (proj_grad,) = whole_call(place_body, "place", [(32, 3 * D)], rows)
    return record_grad[None], proj_grad


def solution(mesh):
    fine = Mesh(mesh.devices.reshape(8, 4, 4, 2), ("z", "y", "x", "core"))
    tm, dp = ("z", "y"), ("x", "core")
    placed = (P(dp, tm, None), P(), P(dp, tm, None))
    return jax.shard_map(
        shards,
        mesh=fine,
        in_specs=placed,
        out_specs=(P(dp, tm, None), P(tm, None)),
        check_vma=False,
    )
```

```python
import functools

import jax
import jax.numpy as jnp
from jax import lax
from jax.experimental import pallas as pl
from jax.experimental.pallas import tpu as pltpu
from jax.sharding import Mesh, PartitionSpec as P

H = 4
HD = 128
CH = 256
NB = 4
D = H * HD
DM = 1024
TOK = NB * CH
F32 = jnp.float32
BF16 = jnp.bfloat16

NN = (((1,), (0,)), ((), ()))
NT = (((1,), (1,)), ((), ()))
TN = (((0,), (0,)), ((), ()))


def dot(a, b, dims):
    return lax.dot_general(a, b, dims, preferred_element_type=F32)


MIB = 1024 * 1024
SWAP = [(0, 1), (1, 0)]


def params(mib=40):
    return pltpu.CompilerParams(vmem_limit_bytes=mib * MIB)


def cost(flops, moved):
    return pl.CostEstimate(flops=int(flops), bytes_accessed=int(moved), transcendentals=0)


def head(part, h):
    return pl.ds(part * D + h * HD, HD)


def project_body(x_ref, w_ref, g_ref, qkv_ref, sg_ref, kv_ref, qg_ref, total_ref):
    n = pl.program_id(0)
    first = (lax.axis_index("z") * 4 + lax.axis_index("y")) * TOK
    qkv_ref[...] = dot(x_ref[...], w_ref[...], NN).astype(BF16)
    pos = (first + n * CH + lax.broadcasted_iota(jnp.int32, (CH, 1), 0)).astype(F32)
    factor = 1.0 / jnp.sqrt(jnp.float32(HD) * (pos + 1.0))
    sg_ref[...] = (g_ref[...].astype(F32) * factor).astype(BF16)

    @pl.when(n == 0)
    def _():
        total_ref[...] = jnp.zeros_like(total_ref)

    for h in range(H):
        kv = dot(qkv_ref[:, head(1, h)], qkv_ref[:, head(2, h)], TN)
        qg = dot(qkv_ref[:, head(0, h)], sg_ref[:, pl.ds(h * HD, HD)], TN)
        kv_ref[0, h] = kv
        qg_ref[0, h] = qg
        total_ref[0, h] += kv
        total_ref[1, h] += qg


def project(x, w, g):
    block = lambda cols: pl.BlockSpec((CH, cols), lambda n: (n, 0))
    sums = pl.BlockSpec((1, H, HD, HD), lambda n: (n, 0, 0, 0))
    return pl.pallas_call(
        project_body,
            grid=(NB,),
            in_specs=[block(DM), pl.BlockSpec((DM, 3 * D), lambda n: (0, 0)), block(D)],
            out_specs=[
                block(3 * D),
                block(D),
                sums,
                sums,
                pl.BlockSpec((2, H, HD, HD), lambda n: (0, 0, 0, 0)),
            ],
        out_shape=[
            jax.ShapeDtypeStruct((TOK, 3 * D), BF16),
            jax.ShapeDtypeStruct((TOK, D), BF16),
            jax.ShapeDtypeStruct((NB, H, HD, HD), F32),
            jax.ShapeDtypeStruct((NB, H, HD, HD), F32),
            jax.ShapeDtypeStruct((2, H, HD, HD), F32),
        ],
        compiler_params=params(60),
        name="project",
    )(x, w, g)


def scan_body(count, v_ref, o_ref):
    back = lax.axis_index("z") >= 4


    def step(t, so_far):
        i = jnp.where(back, count - 1 - t, t)
        o_ref[i] = so_far
        return so_far + v_ref[i]

    lax.fori_loop(0, count, step, jnp.zeros(v_ref.shape[1:], F32))


def scan_states(v):
    return pl.pallas_call(
        functools.partial(scan_body, v.shape[0]),
        in_specs=[pl.BlockSpec(memory_space=pltpu.VMEM)],
        out_specs=pl.BlockSpec(memory_space=pltpu.VMEM),
        out_shape=jax.ShapeDtypeStruct(v.shape, F32),
        compiler_params=params(4),
        name="scan_states",
    )(v)


def local_body(at_ref, qkv_ref, sg_ref, kv_ref, qg_ref, x_hbm, loc_ref, give_ref, from_ref, x_ref, sem):
    n = pl.program_id(0)
    copy = pltpu.make_async_copy(x_hbm, x_ref, sem)
    theirs = pl.multiple_of((1 - at_ref[0]) * 256, 256)

    @pl.when(n == 0)
    def _():
        copy.start()

    @pl.when(n < NB)
    def _():
        keep = lax.broadcasted_iota(jnp.int32, (CH, CH), 0) >= lax.broadcasted_iota(jnp.int32, (CH, CH), 1)
        for h in range(H):
            q, k, v = (qkv_ref[:, head(p, h)] for p in range(3))
            g = sg_ref[:, pl.ds(h * HD, HD)]
            before = jnp.zeros((HD, HD), F32)
            after = jnp.zeros((HD, HD), F32)
            for m in range(NB):
                before = before + jnp.where(m < n, kv_ref[m, h], 0.0)
                after = after + jnp.where(m > n, qg_ref[m, h], 0.0)
            before = before.astype(BF16)
            after = after.astype(BF16)
            mvg = jnp.where(keep, dot(g, v, NT), 0.0).astype(BF16)
            mqk = jnp.where(keep, dot(q, k, NT), 0.0).astype(BF16)
            dq = dot(mvg, k, NN) + dot(g, before, NT)
            dk = dot(mvg, q, TN) + dot(v, after, NT)
            dv = dot(mqk, g, TN) + dot(k, after, NN)
            for p, d in enumerate((dq, dk, dv)):
                loc_ref[:, head(p, h)] = d.astype(BF16)
        rows = pl.ds(pl.multiple_of(n * CH, CH), CH)
        for p in range(3):
            from_ref[rows, p * 256 : (p + 1) * 256] = loc_ref[:, pl.ds(p * D + theirs, 256)]

    @pl.when(n == NB)
    def _():
        copy.wait()

    @pl.when(n >= NB)
    def _():
        half = pl.ds(pl.multiple_of((n - NB) * (DM // 2), DM // 2), DM // 2)
        give_ref[...] = dot(x_ref[:, half], from_ref[...], TN)


def local(at, qkv, sg, kv, qg, x):
    first = lambda n: jnp.minimum(n, NB - 1)
    last = lambda n: jnp.maximum(n - NB, 0)
    block = lambda cols: pl.BlockSpec((CH, cols), lambda n, s: (first(n), 0))
    sums = pl.BlockSpec((NB, H, HD, HD), lambda n, s: (0, 0, 0, 0))
    return pl.pallas_call(
        local_body,
        grid_spec=pltpu.PrefetchScalarGridSpec(
            num_scalar_prefetch=1,
            grid=(NB + 2,),
            in_specs=[
                block(3 * D),
                block(D),
                sums,
                sums,
                pl.BlockSpec(memory_space=pltpu.HBM),
            ],
            out_specs=[block(3 * D), pl.BlockSpec((DM // 2, 768), lambda n, s: (last(n), 0))],
            scratch_shapes=[
                pltpu.VMEM((TOK, 768), BF16),
                pltpu.VMEM((TOK, DM), BF16),
                pltpu.SemaphoreType.DMA,
            ],
        ),
        out_shape=[
            jax.ShapeDtypeStruct((TOK, 3 * D), BF16),
            jax.ShapeDtypeStruct((DM, 768), F32),
        ],
        compiler_params=params(60),
        cost_estimate=cost(8e9, 24e6),
        name="local",
    )(at, qkv, sg, kv, qg, x)


def factors_body(at_ref, x_ref, *refs):
    for j, ref in enumerate(refs[:3]):
        refs[3][:, j * 256 : (j + 1) * 256] = dot(x_ref[...], ref[...], TN)


def factors(at, x, sources):
    cols = [pl.BlockSpec((TOK, 256), lambda i, s, f=f: (0, f + 1 - s[0])) for _, f in sources]
    return pl.pallas_call(
        factors_body,
        grid_spec=pltpu.PrefetchScalarGridSpec(
            num_scalar_prefetch=1,
            grid=(2,),
            in_specs=[pl.BlockSpec((TOK, DM // 2), lambda i, s: (0, i))] + cols,
            out_specs=pl.BlockSpec((DM // 2, 768), lambda i, s: (i, 0)),
        ),
        out_shape=jax.ShapeDtypeStruct((DM, 768), F32),
        compiler_params=params(60),
        cost_estimate=cost(60e9, 12e6),
        name="factors",
    )(at, x, *(a for a, _ in sources))


def keep_body(at_ref, x_ref, r_ref, *refs):
    w_ref, f_ref = refs[6:]
    for j in range(3):
        cols = slice(j * 256, (j + 1) * 256)
        w_ref[:, cols] = dot(x_ref[...], refs[j][...], TN) + r_ref[:, cols]
        f_ref[:, cols] = dot(x_ref[...], refs[3 + j][...], TN).astype(BF16)


def keep(at, x, arrived, sources):
    cols = [pl.BlockSpec((TOK, 256), lambda i, s, f=f: (0, f + s[0])) for _, f in sources]
    rows = pl.BlockSpec((DM // 2, 768), lambda i, s: (i, 0))
    return pl.pallas_call(
        keep_body,
        grid_spec=pltpu.PrefetchScalarGridSpec(
            num_scalar_prefetch=1,
            grid=(2,),
            in_specs=[pl.BlockSpec((TOK, DM // 2), lambda i, s: (0, i)), rows] + cols,
            out_specs=[rows, rows],
        ),
        out_shape=[jax.ShapeDtypeStruct((DM, 768), F32), jax.ShapeDtypeStruct((DM, 768), BF16)],
        compiler_params=params(60),
        cost_estimate=cost(40e9, 16e6),
        name="keep",
    )(at, x, arrived, *(a for a, _ in sources))


def pick(axis):
    mine = lax.axis_index(axis)
    first = jnp.where(lax.axis_index("core") == 0, 1, 3)
    second = 4 - first
    return (mine, mine ^ second), (mine ^ first, mine ^ first ^ second)


def own_body(w_hbm, a_hbm, b_hbm, s_ref, o_ref, far_ref, w_ref, a_ref, b_ref, sems):
    core = lax.axis_index("core")
    copies = []
    for j in range(3):
        cols = pl.ds(j * 256, 256)
        copies.append(
            (
                pltpu.make_async_copy(w_hbm.at[:, cols], w_ref.at[j], sems.at[0, j]),
                pltpu.make_async_copy(a_hbm.at[:, cols], a_ref.at[j], sems.at[1, j]),
                pltpu.make_async_copy(b_hbm.at[:, cols], b_ref.at[j], sems.at[2, j]),
            )
        )
    for group in copies:
        for copy in group:
            copy.start()
    for j, (kind, dims) in enumerate(((0, NT), (1, NT), (1, NN))):
        for copy in copies[j]:
            copy.wait()
        for i in range(2):
            cols = slice(i * HD, (i + 1) * HD)
            term = dot(a_ref[j, :, cols], s_ref[kind, 2 * core + i].astype(BF16), dims)
            o_ref[j, :, cols] = w_ref[j, :, cols] + term
        far_ref[j] = b_ref[j].astype(BF16)


def own_states(w, a, b, states):
    vmem = pl.BlockSpec(memory_space=pltpu.VMEM)
    hbm = pl.BlockSpec(memory_space=pltpu.HBM)
    return pl.pallas_call(
        own_body,
        in_specs=[hbm, hbm, hbm, vmem],
        out_specs=[vmem, vmem],
        out_shape=[
            jax.ShapeDtypeStruct((3, DM, 256), F32),
            jax.ShapeDtypeStruct((3, DM, 256), BF16),
        ],
        scratch_shapes=[
            pltpu.VMEM((3, DM, 256), F32),
            pltpu.VMEM((3, DM, 256), BF16),
            pltpu.VMEM((3, DM, 256), F32),
            pltpu.SemaphoreType.DMA((3, 3)),
        ],
        compiler_params=params(47),
        cost_estimate=cost(5e9, 12e6),
        name="own_states",
    )(w, a, b, states)


def finish_body(w_ref, b_ref, s_ref, kx_ref, sx_ref, ky_ref, sy_ref, t_ref):
    core = lax.axis_index("core")
    for j, (kind, dims) in enumerate(((0, NT), (1, NT), (1, NN))):
        for i in range(2):
            cols = slice(i * HD, (i + 1) * HD)
            term = dot(b_ref[j, :, cols], s_ref[kind, 2 * core + i].astype(BF16), dims)
            t_ref[j, :, :, :, :, cols] = (w_ref[j, :, cols] + term).reshape(8, 4, 4, 8, HD)
        lanes = slice(j * HD, (j + 1) * HD)
        kept, sent = pick("x")
        for i in range(2):
            kx_ref[:, :, i, :, lanes] = t_ref[j, :, :, kept[i], :, 0:128]
            sx_ref[:, :, i, :, lanes] = t_ref[j, :, :, sent[i], :, 0:128]
        kept, sent = pick("y")
        for i in range(2):
            ky_ref[:, i, :, :, lanes] = t_ref[j, :, kept[i], :, :, 128:256]
            sy_ref[:, i, :, :, lanes] = t_ref[j, :, sent[i], :, :, 128:256]


def finish(w, b, states):
    vmem = pl.BlockSpec(memory_space=pltpu.VMEM)
    return pl.pallas_call(
        finish_body,
        in_specs=[vmem] * 3,
        out_specs=[vmem] * 4,
        out_shape=[jax.ShapeDtypeStruct((8, 4, 2, 8, 384), F32)] * 2
        + [jax.ShapeDtypeStruct((8, 2, 4, 8, 384), F32)] * 2,
        scratch_shapes=[pltpu.VMEM((3, 8, 4, 4, 8, 256), F32)],
        compiler_params=params(44),
        cost_estimate=cost(1e9, 12e6),
        name="finish",
    )(w, b, states)


def inputs_body(loc_ref, qkv_ref, sg_ref, s_ref, w_ref, o_ref, d_ref):
    for h in range(H):
        before = s_ref[0, h].astype(BF16)
        after = s_ref[1, h].astype(BF16)
        parts = (
            dot(sg_ref[:, pl.ds(h * HD, HD)], before, NT),
            dot(qkv_ref[:, head(2, h)], after, NT),
            dot(qkv_ref[:, head(1, h)], after, NN),
        )
        for p, d in enumerate(parts):
            d_ref[:, head(p, h)] = (loc_ref[:, head(p, h)].astype(F32) + d).astype(BF16)
    o_ref[...] = dot(d_ref[...], w_ref[...], NT).astype(BF16)


def inputs_grad(loc, qkv, sg, states, weights):
    block = lambda cols: pl.BlockSpec((CH, cols), lambda n: (n, 0))
    return pl.pallas_call(
        inputs_body,
        grid=(NB,),
        in_specs=[
            block(3 * D),
            block(3 * D),
            block(D),
            pl.BlockSpec((2, H, HD, HD), lambda n: (0, 0, 0, 0)),
            pl.BlockSpec((DM, 3 * D), lambda n: (0, 0)),
        ],
        out_specs=block(DM),
        out_shape=jax.ShapeDtypeStruct((TOK, DM), BF16),
        scratch_shapes=[pltpu.VMEM((CH, 3 * D), BF16)],
        compiler_params=params(50),
        cost_estimate=cost(5e9, 14e6),
        name="inputs_grad",
    )(loc, qkv, sg, states, weights)


def whole_call(body, name, shapes, *args, scratch=()):
    vmem = pl.BlockSpec(memory_space=pltpu.VMEM)
    smem = pl.BlockSpec(memory_space=pltpu.SMEM)
    return pl.pallas_call(
        body,
        in_specs=[smem if a.dtype == jnp.int32 else vmem for a in args],
        out_specs=[vmem] * len(shapes),
        out_shape=[jax.ShapeDtypeStruct(s, F32) for s in shapes],
        scratch_shapes=list(scratch),
        compiler_params=params(16),
        name=name,
    )(*args)


def add1_body(k, r, ko, so):
    at = (slice(None), slice(None)) if k.shape[1] == 4 else (slice(None),)
    ko[...] = k[at + (0,)] + r[at + (0,)]
    so[...] = k[at + (1,)] + r[at + (1,)]


def add2_body(axis, k, r, ko, so):
    kept, sent = pick(axis)
    for i in range(2):
        ko[:, i] = k[:, kept[i]] + r[:, kept[i]]
        so[:, i] = k[:, sent[i]] + r[:, sent[i]]


def add3_body(k, r, ko, so):
    ko[...] = k[:, 0] + r[:, 0]
    so[...] = k[:, 1] + r[:, 1]


def add4_body(kp, rp, kq, rq, o):
    o[:, :, 0:384] = kp[...] + rp[...]
    o[:, :, 384:768] = kq[...] + rq[...]


def sum_body(v, o):
    total = v[0]
    for i in range(1, v.shape[0]):
        total = total + v[i]
    for i in range(o.shape[0]):
        o[i] = total


def both_cores_body(mine, other, o):
    core = lax.axis_index("core")
    for i in range(4):
        o[i, core] = mine[0]
        o[i, 1 - core] = other[0]


def place_body(v, o):
    for i in range(8):
        for p in range(6):
            at = (p % 3) * 512 + (i % 2) * 256 + (p // 3) * 128
            o[i // 2 * 8 : i // 2 * 8 + 8, at : at + 128] = v[i, :, p * 128 : (p + 1) * 128]


def exchange(value, axis, step):
    pairs = []
    for i in range(4):
        for c in range(2):
            j = i ^ ((1, 3), (3, 1))[c][step]
            pairs.append((2 * i + c, 2 * j + c))
    return lax.ppermute(value, (axis, "core"), pairs)


def shards(inputs, weights, out_grad):
    x = inputs[0]
    at = lax.axis_index("core").astype(jnp.int32)[None]

    qkv, sg, kv, qg, total = project(x, weights, out_grad[0])
    slices = lax.all_to_all(total.reshape(32, 32, HD), ("z", "y"), 0, 0, tiled=True)
    loc, given = local(at, qkv, sg, kv, qg, x)
    local_in = lax.ppermute(given, "core", SWAP)
    slices, loc = lax.optimization_barrier((slices, loc))
    scanned = scan_states(slices)
    scanned, sg, qkv, loc = lax.optimization_barrier((scanned, sg, qkv, loc))
    states = lax.all_to_all(scanned, ("z", "y"), 0, 0, tiled=True)
    given = factors(at, x, [(sg, 0), (qkv, 4), (qkv, 2)])
    factors_in = lax.ppermute(given, "core", SWAP)
    both, mine = keep(at, x, local_in, [(loc, 0), (loc, 2), (loc, 4), (sg, 0), (qkv, 4), (qkv, 2)])
    states, mine, both = lax.optimization_barrier((states, mine, both))

    states = states.reshape(2, H, HD, HD)
    states_in = lax.ppermute(states, "core", SWAP)
    both, far = own_states(both, mine, factors_in, states)
    kx, sx, ky, sy = finish(both, far, states_in)
    rx = exchange(sx, "x", 0)
    ry = exchange(sy, "y", 0)
    record_grad = inputs_grad(loc, qkv, sg, states, weights)
    rx, ry, record_grad = lax.optimization_barrier((rx, ry, record_grad))
    kp, sp = whole_call(add1_body, "add1x", [(8, 4, 8, 384)] * 2, kx, rx)
    rp = exchange(sp, "x", 1)
    kq, sq = whole_call(add1_body, "add1y", [(8, 4, 8, 384)] * 2, ky, ry)
    rq = exchange(sq, "y", 1)
    kp, sp = whole_call(functools.partial(add2_body, "y"), "add2x", [(8, 2, 8, 384)] * 2, kp, rp)
    rp = exchange(sp, "y", 0)
    kq, sq = whole_call(functools.partial(add2_body, "x"), "add2y", [(8, 2, 8, 384)] * 2, kq, rq)
    rq = exchange(sq, "x", 0)
    kp, sp = whole_call(add3_body, "add3x", [(8, 8, 384)] * 2, kp, rp)
    rp = exchange(sp, "y", 1)
    kq, sq = whole_call(add3_body, "add3y", [(8, 8, 384)] * 2, kq, rq)
    rq = exchange(sq, "x", 1)
    (part,) = whole_call(add4_body, "add4", [(8, 8, 768)], kp, rp, kq, rq)
    part = lax.all_to_all(part, "z", 0, 0, tiled=True)
    (own,) = whole_call(sum_body, "sum_z", [(1, 8, 768)], part)
    other = lax.ppermute(own, "core", SWAP)
    (pair,) = whole_call(both_cores_body, "both_cores", [(4, 2, 8, 768)], own, other)
    rows = lax.all_to_all(pair, "x", 0, 0, tiled=True).reshape(8, 8, 768)
    (proj_grad,) = whole_call(place_body, "place", [(32, 3 * D)], rows)
    return record_grad[None], proj_grad


def solution(mesh):
    fine = Mesh(mesh.devices.reshape(8, 4, 4, 2), ("z", "y", "x", "core"))
    tm, dp = ("z", "y"), ("x", "core")
    placed = (P(dp, tm, None), P(), P(dp, tm, None))
    return jax.shard_map(
        shards,
        mesh=fine,
        in_specs=placed,
        out_specs=(P(dp, tm, None), P(tm, None)),
        check_vma=False,
    )
```
